512 devices in a mesh: chan: 64 (over x, z), tm: 8 (over y, core).
Axes of the slice: x: 4, y: 4, z: 16, core: 2. Of those that a mesh axis runs over, the one named last changes fastest.
Arguments:
- voltages: float32 [512, 3072, 128], P('chan', 'tm'), may hold values from -11 to 11
- steering: int32 [64, 512, 512], P('chan'), may hold values from 0 to 1023
- chirp_phase: float32 [64, 512], P('chan'), may hold values from -3.140625 to 3.140625
- delays: int32 [1, 64], replicated, may hold values from 0 to 383
Outputs:
- trial_spectra: float32 [512, 1, 2, 1024], P('chan', None, None, 'tm')
The draws below stay inside these ranges and needn't reach their ends.
All inputs are finite; a program needn't handle non-finite values.
Results may differ from the reference program's by a relative error of at most 0.00012.
Values sent between devices are 32-bit elements; how exact they have to be, the bound alone decides.
A program may use at most 64 MiB of HBM per device.

```python
import math
import jax
import jax.numpy as jnp
from jax import lax

BEAMS = 512
BLOCK = 384
HALO = 128
FREQ = 128
PHASES = 1024
TRIALS = 1
STATIONS = 512
CHANNELS = 64
SPECTRA = 3072
WINDOW = 512
N_TM = 8


def draw_voltages(key, part):
    key = jax.random.fold_in(key, 11)
    time_index = jnp.arange(SPECTRA, dtype=jnp.float32)
    envelope = jnp.sqrt(1.0 + 2.0 * time_index / (SPECTRA - 1))
    base_draw = jnp.clip(jax.random.normal(key, (STATIONS, SPECTRA, 2 * CHANNELS), jnp.float32), -6.0, 6.0)
    values = base_draw * envelope[None, :, None]
    return values.astype(jnp.float32)


def set_ends(array, rng, smallest, largest):
    spot = [jax.random.randint(jax.random.fold_in(rng, axis), (), 0, length) for axis, length in enumerate(array.shape)]
    widest = array.shape.index(max(array.shape))
    neighbour = spot[:widest] + [(spot[widest] + 1) % array.shape[widest]] + spot[widest + 1:]
    return array.at[tuple(spot)].set(smallest).at[tuple(neighbour)].set(largest)


def setup_inputs(seed: int = 0) -> dict:
    arg_keys = jax.random.split(jax.random.key(seed), 5)
    voltages = draw_voltages(jax.random.fold_in(arg_keys[4], 71), 0)
    steering = set_ends(jax.random.randint(arg_keys[1], (CHANNELS, BEAMS, STATIONS), 0, PHASES), jax.random.fold_in(arg_keys[1], 1), 0, PHASES - 1).astype(jnp.int32)
    chirp_phase = jnp.clip(jax.random.uniform(arg_keys[2], (CHANNELS, WINDOW), jnp.float32, -3.140625, 3.140625), -3.140625, 3.140625)
    delays = set_ends(jax.random.randint(arg_keys[3], (TRIALS, CHANNELS), 0, BLOCK), jax.random.fold_in(arg_keys[3], 1), 0, BLOCK - 1).astype(jnp.int32)
    return {"voltages": voltages, "steering": steering, "chirp_phase": chirp_phase, "delays": delays}


exact_arithmetic = lax.Precision.HIGHEST
epsilon = 1e-06

def angle_tables(row_count, col_count, length, row_first, col_first):
    row_index = jnp.arange(row_count, dtype=jnp.int32)[:, None] + row_first
    col_index = jnp.arange(col_count, dtype=jnp.int32)[None, :] + col_first
    turn_count = row_index * col_index % length
    angles = turn_count.astype(jnp.float32) * (2.0 * math.pi / length)
    return (jnp.cos(angles), jnp.sin(angles))

def channel_table(channels):
    cos_part, sin_part = angle_tables(channels, channels, channels, 0, 0)
    upper_rows = jnp.stack([cos_part, -sin_part], axis=1)
    lower_rows = jnp.stack([sin_part, cos_part], axis=1)
    return jnp.concatenate([upper_rows, lower_rows], axis=0) / math.sqrt(channels)

def steer_matrix(phase_rows, stations):
    angles = phase_rows.astype(jnp.float32) * (2.0 * math.pi / PHASES)
    weight_real = jnp.cos(angles)
    weight_imag = jnp.sin(angles)
    upper_rows = jnp.concatenate([weight_real, -weight_imag], axis=1)
    lower_rows = jnp.concatenate([weight_imag, weight_real], axis=1)
    return jnp.concatenate([upper_rows, lower_rows], axis=0) / math.sqrt(stations)

def forward_matrix(window):
    cos_part, sin_part = angle_tables(window, window, window, 0, 0)
    upper_rows = jnp.concatenate([cos_part, -sin_part], axis=1)
    lower_rows = jnp.concatenate([sin_part, cos_part], axis=1)
    return jnp.concatenate([upper_rows, lower_rows], axis=0)

def inverse_matrix(window, block_len, halo_len):
    cos_part, sin_part = angle_tables(window, block_len, window, 0, halo_len)
    upper_rows = jnp.concatenate([cos_part, sin_part], axis=1)
    lower_rows = jnp.concatenate([-sin_part, cos_part], axis=1)
    return jnp.concatenate([upper_rows, lower_rows], axis=0) / window

def block_matrix(block_len, bin_count):
    cos_part, sin_part = angle_tables(block_len, bin_count, block_len, 0, 1)
    return jnp.concatenate([cos_part, -sin_part], axis=1) / math.sqrt(block_len)

def dedisperse(window_flat, chirp_row, forward_table, inverse_table, block_len):
    window = chirp_row.shape[0]
    spectrum = jnp.dot(window_flat, forward_table, precision=exact_arithmetic)
    spectrum_real = spectrum[:, :window]
    spectrum_imag = spectrum[:, window:]
    chirp_cos = jnp.cos(chirp_row)[None, :]
    chirp_sin = jnp.sin(chirp_row)[None, :]
    shifted_real = spectrum_real * chirp_cos - spectrum_imag * chirp_sin
    shifted_imag = spectrum_real * chirp_sin + spectrum_imag * chirp_cos
    restored = jnp.dot(jnp.concatenate([shifted_real, shifted_imag], axis=1), inverse_table, precision=exact_arithmetic)
    return restored[:, :block_len] ** 2 + restored[:, block_len:] ** 2

def trial_sum(normed, delay_rows, block_table, block_len, channels):
    bin_count = block_table.shape[1] // 2
    spectra = jnp.einsum('cbt,tg->cbg', normed, block_table, precision=exact_arithmetic)
    frequency_real_values = spectra[:, :, :bin_count]
    frequency_imaginary_values = spectra[:, :, bin_count:]
    bin_index = jnp.arange(1, bin_count + 1, dtype=jnp.int32)
    turn_count = delay_rows[:, :, None] * bin_index[None, None, :] % block_len
    angles = turn_count.astype(jnp.float32) * (2.0 * math.pi / block_len)
    phase_shift_cosine = jnp.cos(angles)
    phase_shift_sine = jnp.sin(angles)
    real_component = jnp.einsum('ope,roe->pre', frequency_real_values, phase_shift_cosine, precision=exact_arithmetic) - jnp.einsum('ope,roe->pre', frequency_imaginary_values, phase_shift_sine, precision=exact_arithmetic)
    imaginary_component = jnp.einsum('ope,roe->pre', frequency_real_values, phase_shift_sine, precision=exact_arithmetic) + jnp.einsum('ope,roe->pre', frequency_imaginary_values, phase_shift_cosine, precision=exact_arithmetic)
    return jnp.stack([real_component, imaginary_component], axis=2) / math.sqrt(channels)

def reference(voltages, steering, chirp_phase, delays):
    chan_data = jnp.einsum('stn,nqc->cqst', voltages, channel_table(CHANNELS), precision=exact_arithmetic)
    forward_table = forward_matrix(WINDOW)
    inverse_table = inverse_matrix(WINDOW, BLOCK, HALO)

    def one_channel(inputs):
        station_data, phase_rows, chirp_row = inputs
        stacked = station_data.reshape(2 * STATIONS, SPECTRA)
        formed = jnp.dot(steer_matrix(phase_rows, STATIONS), stacked, precision=exact_arithmetic)
        blocks = formed.reshape(2 * BEAMS, N_TM, BLOCK)
        earlier = jnp.concatenate([jnp.zeros((2 * BEAMS, 1, HALO), jnp.float32), blocks[:, :-1, BLOCK - HALO:]], axis=1)
        windows = jnp.concatenate([earlier, blocks], axis=2)
        window_flat = jnp.concatenate([windows[:BEAMS], windows[BEAMS:]], axis=2)
        window_flat = jnp.transpose(window_flat, (1, 0, 2)).reshape(N_TM * BEAMS, 2 * WINDOW)
        detected = dedisperse(window_flat, chirp_row, forward_table, inverse_table, BLOCK)
        return detected.reshape(N_TM, BEAMS, BLOCK)
    powers = lax.map(one_channel, (chan_data, steering, chirp_phase))
    mean_power = lax.optimization_barrier(jnp.sum(powers, axis=(1, 3))) / SPECTRA
    centred = powers - mean_power[:, None, :, None]
    spread = lax.optimization_barrier(jnp.sum(centred * centred, axis=(1, 3))) / SPECTRA
    normed = centred * lax.rsqrt(spread + epsilon)[:, None, :, None]
    block_table = block_matrix(BLOCK, FREQ)

    def one_block(normed_block):
        return trial_sum(normed_block, delays, block_table, BLOCK, CHANNELS)
    per_block = lax.map(one_block, jnp.transpose(normed, (1, 0, 2, 3)))
    return jnp.transpose(per_block, (1, 2, 3, 0, 4)).reshape(BEAMS, TRIALS, 2, N_TM * FREQ)
```

```python
import math

import jax
import jax.numpy as jnp
from jax import lax
from jax.experimental import pallas as pl
from jax.experimental.pallas import tpu as pltpu
from jax.sharding import PartitionSpec as P

MESH = pl.DeviceIdType.MESH
F32 = jnp.float32
BF16 = jnp.bfloat16

NX, NZ, NT = 4, 16, 8
NC = NX * NZ
BEAMS = 512
STATIONS = 512
PER = STATIONS // NC
ROWS = 2 * PER
CHANNELS = 64
BLOCK = 384
HALO = 128
WINDOW = 512
FREQ = 128
PHASES = 1024
SPECTRA = 3072
T = 128
PARTS = BLOCK // T
SLABS = 2
SB = BEAMS // SLABS
EPSILON = 1e-06
THIRD = (2, 0, 1)


def sincos(turns, period):
    quarter = ((turns + period / 8) * (4.0 / period)).astype(jnp.int32)
    t = (turns - quarter.astype(F32) * (period / 4)) * (2.0 * math.pi / period)
    t2 = t * t
    s = t * (1.0 + t2 * (-1 / 6 + t2 * (1 / 120 + t2 * (-1 / 5040 + t2 * (1 / 362880)))))
    c = 1.0 + t2 * (-1 / 2 + t2 * (1 / 24 + t2 * (-1 / 720 + t2 * (1 / 40320 - t2 * (1 / 3628800)))))
    odd = (quarter & 1) == 1
    cos_part = jnp.where(odd, s, c)
    sin_part = jnp.where(odd, c, s)
    cos_part = jnp.where(((quarter + 1) & 2) == 2, -cos_part, cos_part)
    sin_part = jnp.where((quarter & 2) == 2, -sin_part, sin_part)
    return cos_part, sin_part


def modulo(value, period):
    return value - jnp.floor((value + 0.5) * (1.0 / period)) * period


def iota(shape, dim):
    return lax.broadcasted_iota(jnp.int32, shape, dim)


def halves(x):
    high = x.astype(BF16)
    return high, (x - high.astype(F32)).astype(BF16)


def dot(a, b):
    return jnp.dot(a, b, preferred_element_type=F32)


def dot_rows(a, b):
    return lax.dot_general(a, b, (((1,), (1,)), ((), ())), preferred_element_type=F32)


def kernel(
    volt, steer, chirp, delays, out,
    vbuf, sbuf, cbuf, dbuf, send, recv, w_hi, w_lo, h_hi, h_lo, g_hi, g_lo, gsum,
    acc, last, halo, stat_s, stat_r, spec, xbuf, ybuf, zbuf,
    in_sem, send_sem, recv_sem, halo_sem, stat_ssem, stat_rsem, x_sem, z_sem,
):
    me = lax.axis_index("chan")
    mt = lax.axis_index("tm")
    mx, mz = me // NZ, lax.rem(me, NZ)

    loads = [
        pltpu.make_async_copy(volt.at[:, pl.ds(THIRD[p] * T, T), :], vbuf.at[p], in_sem.at[p])
        for p in range(PARTS)
    ]
    loads += [
        pltpu.make_async_copy(steer.at[0], sbuf, in_sem.at[PARTS]),
        pltpu.make_async_copy(chirp, cbuf, in_sem.at[PARTS + 1]),
        pltpu.make_async_copy(delays, dbuf, in_sem.at[PARTS + 2]),
    ]
    for load in loads:
        load.start()

    barrier = pltpu.get_barrier_semaphore()

    def greet_chan(k, _):
        pl.semaphore_signal(
            barrier, inc=1, device_id={"chan": lax.rem(me + k, NC)}, device_id_type=MESH
        )
        return 0

    def greet_tm(k, _):
        pl.semaphore_signal(
            barrier, inc=1, device_id={"tm": lax.rem(mt + k, NT)}, device_id_type=MESH
        )
        return 0

    lax.fori_loop(1, NC, greet_chan, 0)
    lax.fori_loop(1, NT, greet_tm, 0)

    row, col = iota((2 * CHANNELS, 2 * CHANNELS), 0), iota((2 * CHANNELS, 2 * CHANNELS), 1)
    turns = ((row >> 1) * (col & (CHANNELS - 1))) & (CHANNELS - 1)
    tc, ts = sincos(turns.astype(F32), CHANNELS)
    imag_out, imag_in = (row & 1) == 1, col >= CHANNELS
    table = jnp.where(imag_out == imag_in, tc, jnp.where(imag_out, -ts, ts))
    t_hi, t_lo = halves(table * (1.0 / math.sqrt(CHANNELS)))

    def channelise(p):
        loads[p].wait()
        v_hi, v_lo = halves(vbuf[p].reshape(PER * T, 2 * CHANNELS))
        made = dot_rows(t_hi, v_hi) + dot_rows(t_hi, v_lo) + dot_rows(t_lo, v_hi)
        for s in range(PER):
            send[p, pl.ds(s, 2 * CHANNELS, stride=PER), :] = made[:, s * T : (s + 1) * T]

    def rows_of(c):
        return pl.ds(pl.multiple_of(c * ROWS, ROWS), ROWS)

    def turn(p):
        def one(k, _):
            c = lax.rem(me + k, NC)
            pltpu.make_async_remote_copy(
                src_ref=send.at[p, rows_of(c), :],
                dst_ref=recv.at[p, rows_of(me), :],
                send_sem=send_sem.at[p],
                recv_sem=recv_sem.at[p],
                device_id={"chan": c},
                device_id_type=MESH,
            ).start()
            return 0

        lax.fori_loop(1, NC, one, 0)
        recv[p, rows_of(me), :] = send[p, rows_of(me), :]

    def all_but_own(ref, p):
        return ref.at[p, pl.ds(0, (NC - 1) * ROWS), :]

    with jax.named_scope("channelise"):
        channelise(0)
    with jax.named_scope("greeting"):
        pl.semaphore_wait(barrier, NC - 1 + NT - 1)
    with jax.named_scope("send"):
        turn(0)
        for p in range(1, PARTS):
            channelise(p)
            turn(p)

    with jax.named_scope("steering"):
        loads[PARTS].wait()
        er, ec = iota((STATIONS, 2 * STATIONS), 0), iota((STATIONS, 2 * STATIONS), 1)
        spread = ((ec // ROWS) * PER + (ec & (PER - 1)) == er).astype(F32).astype(BF16)
        rows = 64

        def weigh(j, _):
            at = pl.multiple_of(j * rows, rows)
            index = sbuf[pl.ds(at, rows), :]
            coarse = dot((index >> 5).astype(F32).astype(BF16), spread)
            fine = dot((index & 31).astype(F32).astype(BF16), spread)
            phase = (coarse * 32.0 + fine).astype(jnp.int32)
            column = iota((rows, 2 * STATIONS), 1)
            phase = (phase + ((column >> 3) & 1) * (PHASES // 4)) & (PHASES - 1)
            wc, ws = sincos(phase.astype(F32), PHASES)
            c_hi, c_lo = halves(wc * (1.0 / math.sqrt(STATIONS)))
            s_hi, s_lo = halves(ws * (1.0 / math.sqrt(STATIONS)))
            slab = j // (SB // rows)
            first = pl.multiple_of(lax.rem(j, SB // rows) * rows, rows)
            w_hi[slab, pl.ds(first, rows), :] = c_hi
            w_lo[slab, pl.ds(first, rows), :] = c_lo
            w_hi[slab, pl.ds(SB + first, rows), :] = s_hi
            w_lo[slab, pl.ds(SB + first, rows), :] = s_lo
            return 0

        lax.fori_loop(0, BEAMS // rows, weigh, 0)

    with jax.named_scope("filter"):
        loads[PARTS + 1].wait()
        chirp_row = cbuf[...]
        pair = jnp.where(
            iota((8, WINDOW), 0) == 0,
            jnp.broadcast_to(jnp.cos(chirp_row), (8, WINDOW)),
            jnp.broadcast_to(jnp.sin(chirp_row), (8, WINDOW)),
        )
        turns = (iota((WINDOW, WINDOW), 0) * iota((WINDOW, WINDOW), 1)) & (WINDOW - 1)
        fc, fs = sincos(turns.astype(F32), WINDOW)
        by_cos = jnp.dot(pair, fc, precision=lax.Precision.HIGHEST, preferred_element_type=F32)
        by_sin = jnp.dot(pair, fs, precision=lax.Precision.HIGHEST, preferred_element_type=F32)
        h_re = (by_cos[0:1] - by_sin[1:2]) * (1.0 / WINDOW)
        h_im = (by_sin[0:1] + by_cos[1:2]) * (1.0 / WINDOW)
        for k in range(WINDOW // T):
            def rolled(h):
                full = pltpu.roll(jnp.broadcast_to(h, (T, WINDOW)), k * T, 1, stride=1, stride_axis=0)
                return full[:, HALO:]

            r_hi, r_lo = halves(rolled(h_re))
            i_hi, i_lo = halves(rolled(h_im))
            for ref, re, im in ((h_hi, r_hi, i_hi), (h_lo, r_lo, i_lo)):
                ref[k, 0:T, 0:BLOCK] = re
                ref[k, 0:T, BLOCK:] = im
                ref[k, T:, 0:BLOCK] = -im
                ref[k, T:, BLOCK:] = re

    with jax.named_scope("transform"):
        loads[PARTS + 2].wait()
        own = iota((1, CHANNELS), 1) == me
        delay = jnp.sum(jnp.where(own, dbuf[...], 0).astype(F32), axis=1, keepdims=True)
        shape = (BLOCK, FREQ)
        moved = iota(shape, 0).astype(F32) - delay + BLOCK
        turns = modulo(moved, BLOCK) * (iota(shape, 1) + 1).astype(F32)
        gc, gs = sincos(modulo(turns, BLOCK), BLOCK)
        g = jnp.concatenate([gc, -gs], axis=1) * (1.0 / math.sqrt(BLOCK * CHANNELS))
        gsum[...] = jnp.sum(g, axis=0, keepdims=True)
        g_high, g_low = halves(g)
        g_hi[...] = g_high
        g_lo[...] = g_low

    def form(p):
        r_hi, r_lo = halves(recv[p])
        both = jnp.concatenate([r_hi, r_lo], axis=1)
        for i in range(SLABS):
            wide = dot(w_hi[i], both)
            yield i, wide[:, :T] + wide[:, T:] + dot(w_lo[i], r_hi)

    def convolve(u, k):
        x_hi, x_lo = halves(jnp.concatenate([u[:SB], u[SB:]], axis=1))
        return dot(x_hi, h_hi[k]) + dot(x_lo, h_hi[k]) + dot(x_hi, h_lo[k])

    def arrived(p):
        pltpu.make_async_copy(all_but_own(send, p), all_but_own(recv, p), recv_sem.at[p]).wait()

    with jax.named_scope("wait_part"):
        arrived(0)
    with jax.named_scope("beams"):
        for i, u in form(0):
            last[i] = u
        give = pltpu.make_async_remote_copy(
            src_ref=last,
            dst_ref=halo,
            send_sem=halo_sem.at[0],
            recv_sem=halo_sem.at[1],
            device_id={"tm": lax.rem(mt + 1, NT)},
            device_id_type=MESH,
        )
        give.start()
        for i in range(SLABS):
            acc[i] = convolve(last[i], THIRD[0] + 1)
    with jax.named_scope("wait_part"):
        arrived(1)
    with jax.named_scope("beams"):
        for i, u in form(1):
            acc[i] += convolve(u, THIRD[1] + 1)
        give.wait_recv()
        for i in range(SLABS):
            acc[i] += convolve(jnp.where(mt > 0, halo[i], 0.0), 0)
    with jax.named_scope("wait_part"):
        arrived(2)

    def give_stat(i, k):
        return pltpu.make_async_remote_copy(
            src_ref=stat_s.at[i],
            dst_ref=stat_r.at[i, mt],
            send_sem=stat_ssem.at[i],
            recv_sem=stat_rsem.at[i],
            device_id={"tm": lax.rem(mt + k, NT)},
            device_id_type=MESH,
        )

    with jax.named_scope("detect"):
        for i, u in form(2):
            v = acc[i] + convolve(u, THIRD[2] + 1)
            power = v[:, :BLOCK] * v[:, :BLOCK] + v[:, BLOCK:] * v[:, BLOCK:]
            mean = jnp.sum(power, axis=1, keepdims=True) * (1.0 / BLOCK)
            centred = power - mean
            square = jnp.sum(centred * centred, axis=1, keepdims=True)
            lane = iota((SB, 128), 1)
            stat = jnp.where(lane == 0, mean, jnp.where(lane == 1, square, 0.0))
            stat_s[i] = stat.T[0:8]
            for k in range(1, NT):
                give_stat(i, k).start()
            stat_r[i, mt] = stat_s[i]
            c_hi, c_lo = halves(centred)
            spec[pl.ds(i * SB, SB), :] = dot(c_hi, g_hi[...]) + dot(c_lo, g_hi[...]) + dot(c_hi, g_lo[...])

    xrows = BEAMS // NX
    with jax.named_scope("scale"):
        for i in range(SLABS):
            rest = stat_r.at[i, pl.ds(0, NT - 1)]
            pltpu.make_async_copy(rest, rest, stat_rsem.at[i]).wait()
            total = stat_r[i, 0]
            for j in range(1, NT):
                total = total + stat_r[i, j]
            mean = total[0:1] * (1.0 / NT)
            square = total[1:2]
            for j in range(NT):
                apart = stat_r[i, j][0:1] - mean
                square = square + apart * apart * float(BLOCK)
            scale = lax.rsqrt(square * (1.0 / SPECTRA) + EPSILON)
            shift = stat_s[i][0:1] - mean
            line = iota((128, SB), 0)
            turned = jnp.where(line == 0, scale, jnp.where(line == 1, shift, 0.0)).T
            rows_i = pl.ds(i * SB, SB)
            spec[rows_i, :] = (spec[rows_i, :] + turned[:, 1:2] * gsum[...]) * turned[:, 0:1]
            for x in range(i * SB // xrows, (i + 1) * SB // xrows):
                @pl.when(mx != x)
                def _(x=x):
                    pltpu.make_async_remote_copy(
                        src_ref=spec.at[pl.ds(x * xrows, xrows), :],
                        dst_ref=xbuf.at[mx],
                        send_sem=x_sem.at[0],
                        recv_sem=x_sem.at[1],
                        device_id={"chan": x * NZ + mz},
                        device_id_type=MESH,
                    ).start()

                @pl.when(mx == x)
                def _(x=x):
                    xbuf[x] = spec[pl.ds(x * xrows, xrows), :]

    with jax.named_scope("sum_x"):
        rest_x = xbuf.at[pl.ds(0, NX - 1)]
        pltpu.make_async_copy(rest_x, rest_x, x_sem.at[1]).wait()
        ybuf[...] = (xbuf[0] + xbuf[1]) + (xbuf[2] + xbuf[3])
        share = xrows // NZ

        def hand(k, _):
            z = lax.rem(mz + k, NZ)
            pltpu.make_async_remote_copy(
                src_ref=ybuf.at[pl.ds(pl.multiple_of(z * share, share), share), :],
                dst_ref=zbuf.at[mz],
                send_sem=z_sem.at[0],
                recv_sem=z_sem.at[1],
                device_id={"chan": mx * NZ + z},
                device_id_type=MESH,
            ).start()
            return 0

        lax.fori_loop(1, NZ, hand, 0)
        zbuf[mz] = ybuf[pl.ds(pl.multiple_of(mz * share, share), share), :]
    with jax.named_scope("sum_z"):
        rest_z = zbuf.at[pl.ds(0, NZ - 1)]
        pltpu.make_async_copy(rest_z, rest_z, z_sem.at[1]).wait()
        total = zbuf[0]
        for j in range(1, NZ):
            total = total + zbuf[j]
        out[:, 0, 0, :] = total[:, :FREQ]
        out[:, 0, 1, :] = total[:, FREQ:]

    with jax.named_scope("drain"):
        for p in range(PARTS):
            pltpu.make_async_copy(all_but_own(send, p), all_but_own(send, p), send_sem.at[p]).wait()
        give.wait_send()
        for i in range(SLABS):
            rest = stat_r.at[i, pl.ds(0, NT - 1)]
            pltpu.make_async_copy(rest, rest, stat_ssem.at[i]).wait()
        pltpu.make_async_copy(rest_x, rest_x, x_sem.at[0]).wait()
        pltpu.make_async_copy(rest_z, rest_z, z_sem.at[0]).wait()


def local(voltages, steering, chirp_phase, delays):
    vmem, sem = pltpu.VMEM, pltpu.SemaphoreType.DMA
    return pl.pallas_call(
        kernel,
        out_shape=jax.ShapeDtypeStruct((BEAMS // NC, 1, 2, FREQ), F32),
        in_specs=[pl.BlockSpec(memory_space=pl.ANY)] * 4,
        out_specs=pl.BlockSpec(memory_space=pltpu.VMEM),
        scratch_shapes=[
            vmem((PARTS, PER, T, 2 * CHANNELS), F32),
            vmem((BEAMS, STATIONS), jnp.int32),
            vmem((1, WINDOW), F32),
            vmem((1, CHANNELS), jnp.int32),
            vmem((PARTS, NC * ROWS, T), F32),
            vmem((PARTS, NC * ROWS, T), F32),
            vmem((SLABS, 2 * SB, 2 * STATIONS), BF16),
            vmem((SLABS, 2 * SB, 2 * STATIONS), BF16),
            vmem((WINDOW // T, 2 * T, 2 * BLOCK), BF16),
            vmem((WINDOW // T, 2 * T, 2 * BLOCK), BF16),
            vmem((BLOCK, 2 * FREQ), BF16),
            vmem((BLOCK, 2 * FREQ), BF16),
            vmem((1, 2 * FREQ), F32),
            vmem((SLABS, SB, 2 * BLOCK), F32),
            vmem((SLABS, 2 * SB, T), F32),
            vmem((SLABS, 2 * SB, T), F32),
            vmem((SLABS, 8, SB), F32),
            vmem((SLABS, NT, 8, SB), F32),
            vmem((BEAMS, 2 * FREQ), F32),
            vmem((NX, BEAMS // NX, 2 * FREQ), F32),
            vmem((BEAMS // NX, 2 * FREQ), F32),
            vmem((NZ, BEAMS // NC, 2 * FREQ), F32),
            sem((PARTS + 3,)),
            sem((PARTS,)),
            sem((PARTS,)),
            sem((2,)),
            sem((SLABS,)),
            sem((SLABS,)),
            sem((2,)),
            sem((2,)),
        ],
        compiler_params=pltpu.CompilerParams(
            collective_id=0, has_side_effects=True, vmem_limit_bytes=48 << 20
        ),
    )(voltages, steering, chirp_phase, delays)


def solution(mesh):
    in_specs = (P("chan", "tm", None), P("chan", None, None), P("chan", None), P())
    out_specs = P("chan", None, None, "tm")
    return jax.shard_map(local, mesh=mesh, in_specs=in_specs, out_specs=out_specs, check_vma=False)
```

```python
import math

import jax
import jax.numpy as jnp
from jax import lax
from jax.experimental import pallas as pl
from jax.experimental.pallas import tpu as pltpu
from jax.sharding import PartitionSpec as P

MESH = pl.DeviceIdType.MESH
F32 = jnp.float32
BF16 = jnp.bfloat16

NX, NZ, NT = 4, 16, 8
NC = NX * NZ
BEAMS = 512
STATIONS = 512
PER = STATIONS // NC
ROWS = 2 * PER
CHANNELS = 64
BLOCK = 384
HALO = 128
WINDOW = 512
FREQ = 128
PHASES = 1024
SPECTRA = 3072
T = 128
PARTS = BLOCK // T
SLABS = 2
SB = BEAMS // SLABS
XROWS = SB // NX
SHARE = BEAMS // NC
GROUPS = 4
MEMBERS = NC // GROUPS
EPSILON = 1e-06
THIRD = (2, 0, 1)


def shift_of(i):
    j = i >> 2
    half = (j + 1) >> 1
    dz = (NZ // 2 + half * (1 - 2 * (j & 1))) & (NZ - 1)
    return ((i & 3) + 1) & (NX - 1), dz


def sincos(turns, period):
    quarter = ((turns + period / 8) * (4.0 / period)).astype(jnp.int32)
    t = (turns - quarter.astype(F32) * (period / 4)) * (2.0 * math.pi / period)
    t2 = t * t
    s = t * (1.0 + t2 * (-1 / 6 + t2 * (1 / 120 + t2 * (-1 / 5040 + t2 * (1 / 362880)))))
    c = 1.0 + t2 * (-1 / 2 + t2 * (1 / 24 + t2 * (-1 / 720 + t2 * (1 / 40320 - t2 * (1 / 3628800)))))
    odd = (quarter & 1) == 1
    cos_part = jnp.where(odd, s, c)
    sin_part = jnp.where(odd, c, s)
    cos_part = jnp.where(((quarter + 1) & 2) == 2, -cos_part, cos_part)
    sin_part = jnp.where((quarter & 2) == 2, -sin_part, sin_part)
    return cos_part, sin_part


def modulo(value, period):
    return value - jnp.floor((value + 0.5) * (1.0 / period)) * period


def iota(shape, dim):
    return lax.broadcasted_iota(jnp.int32, shape, dim)


def halves(x):
    high = x.astype(BF16)
    return high, (x - high.astype(F32)).astype(BF16)


def dot(a, b):
    return jnp.dot(a, b, preferred_element_type=F32)


def dot_rows(a, b):
    return lax.dot_general(a, b, (((1,), (1,)), ((), ())), preferred_element_type=F32)


def kernel(
    volt, steer, chirp, delays, out,
    vbuf, sbuf, cbuf, dbuf, send, recv, w_hi, w_lo, h_hi, h_lo, g_hi, g_lo, gsum,
    acc, last, halo, beams, stat_s, stat_r, spec, xbuf, ybuf, zbuf,
    in_sem, send_sem, recv_sem, halo_sem, stat_sem, x_ssem, x_rsem, z_sem,
):
    me = lax.axis_index("chan")
    mt = lax.axis_index("tm")
    mx, mz = me // NZ, lax.rem(me, NZ)

    loads = [
        pltpu.make_async_copy(volt.at[:, pl.ds(THIRD[p] * T, T), :], vbuf.at[p], in_sem.at[p])
        for p in range(PARTS)
    ]
    loads += [
        pltpu.make_async_copy(steer.at[0], sbuf, in_sem.at[PARTS]),
        pltpu.make_async_copy(chirp, cbuf, in_sem.at[PARTS + 1]),
        pltpu.make_async_copy(delays, dbuf, in_sem.at[PARTS + 2]),
    ]
    for load in loads:
        load.start()

    barrier = pltpu.get_barrier_semaphore()

    def peer(i):
        dx, dz = shift_of(i)
        return ((mx + dx) & (NX - 1)) * NZ + ((mz + dz) & (NZ - 1))

    def greet_chan(i, _):
        pl.semaphore_signal(barrier, inc=1, device_id={"chan": peer(i)}, device_id_type=MESH)
        return 0

    def relative(i):
        dx, dt = ((i >> 3) + 1) & (NX - 1), ((i & (NT - 1)) + 1) & (NT - 1)
        return ((mx + dx) & (NX - 1)), {
            "chan": ((mx + dx) & (NX - 1)) * NZ + mz,
            "tm": (mt + dt) & (NT - 1),
        }

    def greet_row(i, _):
        @pl.when((i & (NT - 1)) != NT - 1)
        def _():
            pl.semaphore_signal(barrier, inc=1, device_id=relative(i)[1], device_id_type=MESH)

        return 0

    lax.fori_loop(0, NC - 1, greet_chan, 0)
    lax.fori_loop(0, NX * NT - 1, greet_row, 0)

    row, col = iota((2 * CHANNELS, 2 * CHANNELS), 0), iota((2 * CHANNELS, 2 * CHANNELS), 1)
    turns = ((row >> 1) * (col & (CHANNELS - 1))) & (CHANNELS - 1)
    tc, ts = sincos(turns.astype(F32), CHANNELS)
    imag_out, imag_in = (row & 1) == 1, col >= CHANNELS
    table = jnp.where(imag_out == imag_in, tc, jnp.where(imag_out, -ts, ts))
    t_hi, t_lo = halves(table * (1.0 / math.sqrt(CHANNELS)))

    def channelise(p):
        loads[p].wait()
        v_hi, v_lo = halves(vbuf[p].reshape(PER * T, 2 * CHANNELS))
        made = dot_rows(t_hi, v_hi) + dot_rows(t_hi, v_lo) + dot_rows(t_lo, v_hi)
        for s in range(PER):
            send[p, pl.ds(s, 2 * CHANNELS, stride=PER), :] = made[:, s * T : (s + 1) * T]

    def rows_of(c):
        return pl.ds(pl.multiple_of(c * ROWS, ROWS), ROWS)

    def turn(p):
        def one(i, _):
            c = peer(i)
            pltpu.make_async_remote_copy(
                src_ref=send.at[p, rows_of(c), :],
                dst_ref=recv.at[p, rows_of(i), :],
                send_sem=send_sem.at[p],
                recv_sem=recv_sem.at[p, i // MEMBERS],
                device_id={"chan": c},
                device_id_type=MESH,
            ).start()
            return 0

        lax.fori_loop(0, NC - 1, one, 0)
        recv[p, rows_of(NC - 1), :] = send[p, rows_of(me), :]

    def all_but_own(ref, p):
        return ref.at[p, pl.ds(0, (NC - 1) * ROWS), :]

    with jax.named_scope("channelise"):
        channelise(0)
    with jax.named_scope("greeting"):
        pl.semaphore_wait(barrier, NC - 1 + NX * (NT - 1))
    with jax.named_scope("send"):
        turn(0)
        for p in range(1, PARTS):
            channelise(p)
            turn(p)

    with jax.named_scope("steering"):
        loads[PARTS].wait()
        er, ec = iota((STATIONS, 2 * STATIONS), 0), iota((STATIONS, 2 * STATIONS), 1)
        dx, dz = shift_of(ec // ROWS)
        sender = ((mx - dx) & (NX - 1)) * NZ + ((mz - dz) & (NZ - 1))
        spread = (sender * PER + (ec & (PER - 1)) == er).astype(F32).astype(BF16)
        rows = 64

        def weigh(j, _):
            at = pl.multiple_of(j * rows, rows)
            index = sbuf[pl.ds(at, rows), :].reshape(rows // 2 // SHARE, 2, SHARE, STATIONS)
            index = jnp.concatenate(
                [index[:, slab].reshape(rows // 2, STATIONS) for slab in range(SLABS)], axis=0
            )
            coarse = dot((index >> 5).astype(F32).astype(BF16), spread)
            fine = dot((index & 31).astype(F32).astype(BF16), spread)
            phase = (coarse * 32.0 + fine).astype(jnp.int32)
            column = iota((rows, 2 * STATIONS), 1)
            phase = (phase + ((column >> 3) & 1) * (PHASES // 4)) & (PHASES - 1)
            wc, ws = sincos(phase.astype(F32), PHASES)
            c_hi, c_lo = halves(wc * (1.0 / math.sqrt(STATIONS)))
            s_hi, s_lo = halves(ws * (1.0 / math.sqrt(STATIONS)))
            first = pl.multiple_of(j * (rows // 2), rows // 2)
            for slab in range(SLABS):
                part = slice(slab * (rows // 2), (slab + 1) * (rows // 2))
                w_hi[slab, pl.ds(first, rows // 2), :] = c_hi[part]
                w_lo[slab, pl.ds(first, rows // 2), :] = c_lo[part]
                w_hi[slab, pl.ds(SB + first, rows // 2), :] = s_hi[part]
                w_lo[slab, pl.ds(SB + first, rows // 2), :] = s_lo[part]
            return 0

        lax.fori_loop(0, BEAMS // rows, weigh, 0)

    with jax.named_scope("filter"):
        loads[PARTS + 1].wait()
        chirp_row = cbuf[...]
        pair = jnp.where(
            iota((8, WINDOW), 0) == 0,
            jnp.broadcast_to(jnp.cos(chirp_row), (8, WINDOW)),
            jnp.broadcast_to(jnp.sin(chirp_row), (8, WINDOW)),
        )
        turns = (iota((WINDOW, WINDOW), 0) * iota((WINDOW, WINDOW), 1)) & (WINDOW - 1)
        fc, fs = sincos(turns.astype(F32), WINDOW)
        by_cos = jnp.dot(pair, fc, precision=lax.Precision.HIGHEST, preferred_element_type=F32)
        by_sin = jnp.dot(pair, fs, precision=lax.Precision.HIGHEST, preferred_element_type=F32)
        h_re = (by_cos[0:1] - by_sin[1:2]) * (1.0 / WINDOW)
        h_im = (by_sin[0:1] + by_cos[1:2]) * (1.0 / WINDOW)
        for k in range(WINDOW // T):
            def rolled(h):
                full = pltpu.roll(jnp.broadcast_to(h, (T, WINDOW)), k * T, 1, stride=1, stride_axis=0)
                return full[:, HALO:]

            r_hi, r_lo = halves(rolled(h_re))
            i_hi, i_lo = halves(rolled(h_im))
            for ref, re, im in ((h_hi, r_hi, i_hi), (h_lo, r_lo, i_lo)):
                ref[k, 0:T, 0:BLOCK] = re
                ref[k, 0:T, BLOCK:] = im
                ref[k, T:, 0:BLOCK] = -im
                ref[k, T:, BLOCK:] = re

    with jax.named_scope("transform"):
        loads[PARTS + 2].wait()
        own = iota((1, CHANNELS), 1) == me
        delay = jnp.sum(jnp.where(own, dbuf[...], 0).astype(F32), axis=1, keepdims=True)
        shape = (BLOCK, FREQ)
        moved = iota(shape, 0).astype(F32) - delay + BLOCK
        turns = modulo(moved, BLOCK) * (iota(shape, 1) + 1).astype(F32)
        gc, gs = sincos(modulo(turns, BLOCK), BLOCK)
        g = jnp.concatenate([gc, -gs], axis=1) * (1.0 / math.sqrt(BLOCK * CHANNELS))
        gsum[...] = jnp.sum(g, axis=0, keepdims=True)
        g_high, g_low = halves(g)
        g_hi[...] = g_high
        g_lo[...] = g_low

    def form(p, into):
        for g in range(GROUPS):
            size = MEMBERS * ROWS
            there = recv.at[p, pl.ds(g * size, size - ROWS if g == GROUPS - 1 else size), :]
            pltpu.make_async_copy(there, there, recv_sem.at[p, g]).wait()
            columns = pl.ds(g * size, size)
            r_hi, r_lo = halves(recv[p, columns, :])
            both = jnp.concatenate([r_hi, r_lo], axis=1)
            for i in range(SLABS):
                wide = dot(w_hi[i, :, columns], both)
                made = wide[:, :T] + wide[:, T:] + dot(w_lo[i, :, columns], r_hi)
                into[i] = made if g == 0 else into[i] + made

    def convolve(u, k):
        x_hi, x_lo = halves(jnp.concatenate([u[:SB], u[SB:]], axis=1))
        return dot(x_hi, h_hi[k]) + dot(x_lo, h_hi[k]) + dot(x_hi, h_lo[k])

    with jax.named_scope("beams"):
        form(0, last)
        give = pltpu.make_async_remote_copy(
            src_ref=last,
            dst_ref=halo,
            send_sem=halo_sem.at[0],
            recv_sem=halo_sem.at[1],
            device_id={"tm": (mt + 1) & (NT - 1)},
            device_id_type=MESH,
        )
        give.start()
        for i in range(SLABS):
            acc[i] = convolve(last[i], THIRD[0] + 1)
        form(1, beams)
        for i in range(SLABS):
            acc[i] += convolve(beams[i], THIRD[1] + 1)
        give.wait_recv()
        for i in range(SLABS):
            acc[i] += convolve(jnp.where(mt > 0, halo[i], 0.0), 0)
        form(2, beams)

    def stat_tiles(power_stats):
        lane = iota((8, 128), 1)
        for x in range(NX):
            tile = [a[:, x // 2 * 128 : (x // 2 + 1) * 128] for a in power_stats]
            if x % 2 == 0:
                tile[1] = pltpu.roll(tile[1], XROWS, 1)
            else:
                tile[0] = pltpu.roll(tile[0], XROWS, 1)
            stat_s[x, 0:2, :] = jnp.where(lane < XROWS, tile[0], tile[1])[0:2]
            stat_s[x, 2:3, :] = gsum[:, :FREQ]
            stat_s[x, 3:4, :] = gsum[:, FREQ:]

    def hand_x(i):
        for dx in (2, 1, 3):
            x = (mx + dx) & (NX - 1)
            pltpu.make_async_remote_copy(
                src_ref=spec.at[i, pl.ds(pl.multiple_of(x * XROWS, XROWS), XROWS), :],
                dst_ref=xbuf.at[i, mx],
                send_sem=x_ssem.at[i],
                recv_sem=x_rsem.at[i],
                device_id={"chan": x * NZ + mz},
                device_id_type=MESH,
            ).start()

    def detect(i):
        v = acc[i] + convolve(beams[i], THIRD[2] + 1)
        power = v[:, :BLOCK] * v[:, :BLOCK] + v[:, BLOCK:] * v[:, BLOCK:]
        mean = jnp.sum(power, axis=1, keepdims=True) * (1.0 / BLOCK)
        return mean, power - mean

    def transform(i, centred):
        c_hi, c_lo = halves(centred)
        spec[i] = dot(c_hi, g_hi[...]) + dot(c_lo, g_hi[...]) + dot(c_hi, g_lo[...])

    def stat_rows(mean, centred):
        square = jnp.sum(centred * centred, axis=1, keepdims=True)
        lane = iota((SB, 128), 1)
        return jnp.where(lane == 0, mean, jnp.where(lane == 1, square, 0.0)).T[0:8]

    def give_stat(i, _):
        x, device = relative(i)
        pltpu.make_async_remote_copy(
            src_ref=stat_s.at[x],
            dst_ref=stat_r.at[mx * NT + mt],
            send_sem=stat_sem.at[0],
            recv_sem=stat_sem.at[1],
            device_id=device,
            device_id_type=MESH,
        ).start()
        return 0

    with jax.named_scope("detect"):
        mean_0, centred_0 = detect(0)
        transform(0, centred_0)
        hand_x(0)
        mean_1, centred_1 = detect(1)
        stat_tiles([stat_rows(mean_0, centred_0), stat_rows(mean_1, centred_1)])
        lax.fori_loop(0, NX * NT - 1, give_stat, 0)
        transform(1, centred_1)
        hand_x(1)
        stat_r[mx * NT + mt] = stat_s[mx]
        for i in range(SLABS):
            xbuf[i, mx] = spec[i, pl.ds(pl.multiple_of(mx * XROWS, XROWS), XROWS), :]

    with jax.named_scope("drain"):
        for p in range(PARTS):
            pltpu.make_async_copy(all_but_own(send, p), all_but_own(send, p), send_sem.at[p]).wait()
        give.wait_send()

    with jax.named_scope("scale"):
        rest_stat = stat_r.at[pl.ds(0, NX * NT - 1)]
        pltpu.make_async_copy(rest_stat, rest_stat, stat_sem.at[1]).wait()
        line = iota((128, 128), 0)
        lines = jnp.zeros((128, 128), F32)
        sums = []
        for x in range(NX):
            stats = [stat_r[x * NT + j] for j in range(NT)]
            total = stats[0]
            for j in range(1, NT):
                total = total + stats[j]
            mean = total[0:1] * (1.0 / NT)
            square = total[1:2]
            for j in range(NT):
                apart = stats[j][0:1] - mean
                square = square + apart * apart * float(BLOCK)
            scale = lax.rsqrt(square * (1.0 / SPECTRA) + EPSILON)
            own = stat_r[x * NT + mt]
            lines = jnp.where(line == 2 * x, scale, lines)
            lines = jnp.where(line == 2 * x + 1, own[0:1] - mean, lines)
            sums.append(jnp.concatenate([own[2:3], own[3:4]], axis=1))
        turned = lines.T

    with jax.named_scope("sum_x"):
        for i in range(SLABS):
            rest_x = xbuf.at[i, pl.ds(0, NX - 1)]
            pltpu.make_async_copy(rest_x, rest_x, x_rsem.at[i]).wait()
            mine = turned[i * XROWS : (i + 1) * XROWS]
            total = None
            for x in range(NX):
                shift, scale = mine[:, 2 * x + 1 : 2 * x + 2], mine[:, 2 * x : 2 * x + 1]
                term = (xbuf[i, x] + shift * sums[x]) * scale
                total = term if x == 0 else total + term
            ybuf[i] = total
            odd = (mz + i) & 1

            def share_of(z):
                return ybuf.at[i, pl.ds(pl.multiple_of((z >> 1) * SHARE, SHARE), SHARE), :]

            def hand(z):
                pltpu.make_async_remote_copy(
                    src_ref=share_of(z),
                    dst_ref=zbuf.at[mz],
                    send_sem=z_sem.at[0],
                    recv_sem=z_sem.at[1],
                    device_id={"chan": mx * NZ + z},
                    device_id_type=MESH,
                ).start()

            for dz in (8, 6, 10, 4, 12, 2, 14):
                hand((mz + dz + odd) & (NZ - 1))

            @pl.when(odd == 1)
            def _():
                hand((mz + 1) & (NZ - 1))

            @pl.when(odd == 0)
            def _():
                zbuf[mz] = share_of(mz)[...]

    with jax.named_scope("sum_z"):
        rest_z = zbuf.at[pl.ds(0, NZ - 1)]
        pltpu.make_async_copy(rest_z, rest_z, z_sem.at[1]).wait()
        total = zbuf[0]
        for j in range(1, NZ):
            total = total + zbuf[j]
        out[:, 0, 0, :] = total[:, :FREQ]
        out[:, 0, 1, :] = total[:, FREQ:]
        for i in range(SLABS):
            rest_x = xbuf.at[i, pl.ds(0, NX - 1)]
            pltpu.make_async_copy(rest_x, rest_x, x_ssem.at[i]).wait()
        pltpu.make_async_copy(rest_stat, rest_stat, stat_sem.at[0]).wait()
        pltpu.make_async_copy(rest_z, rest_z, z_sem.at[0]).wait()


def local(voltages, steering, chirp_phase, delays):
    vmem, sem = pltpu.VMEM, pltpu.SemaphoreType.DMA
    return pl.pallas_call(
        kernel,
        out_shape=jax.ShapeDtypeStruct((BEAMS // NC, 1, 2, FREQ), F32),
        in_specs=[pl.BlockSpec(memory_space=pltpu.HBM)] * 4,
        out_specs=pl.BlockSpec(memory_space=pltpu.VMEM),
        scratch_shapes=[
            vmem((PARTS, PER, T, 2 * CHANNELS), F32),
            vmem((BEAMS, STATIONS), jnp.int32),
            vmem((1, WINDOW), F32),
            vmem((1, CHANNELS), jnp.int32),
            vmem((PARTS, NC * ROWS, T), F32),
            vmem((PARTS, NC * ROWS, T), F32),
            vmem((SLABS, 2 * SB, 2 * STATIONS), BF16),
            vmem((SLABS, 2 * SB, 2 * STATIONS), BF16),
            vmem((WINDOW // T, 2 * T, 2 * BLOCK), BF16),
            vmem((WINDOW // T, 2 * T, 2 * BLOCK), BF16),
            vmem((BLOCK, 2 * FREQ), BF16),
            vmem((BLOCK, 2 * FREQ), BF16),
            vmem((1, 2 * FREQ), F32),
            vmem((SLABS, SB, 2 * BLOCK), F32),
            vmem((SLABS, 2 * SB, T), F32),
            vmem((SLABS, 2 * SB, T), F32),
            vmem((SLABS, 2 * SB, T), F32),
            vmem((NX, 4, 128), F32),
            vmem((NX * NT, 4, 128), F32),
            vmem((SLABS, SB, 2 * FREQ), F32),
            vmem((SLABS, NX, XROWS, 2 * FREQ), F32),
            vmem((SLABS, XROWS, 2 * FREQ), F32),
            vmem((NZ, SHARE, 2 * FREQ), F32),
            sem((PARTS + 3,)),
            sem((PARTS,)),
            sem((PARTS, GROUPS)),
            sem((2,)),
            sem((2,)),
            sem((SLABS,)),
            sem((SLABS,)),
            sem((2,)),
        ],
        compiler_params=pltpu.CompilerParams(
            collective_id=0, has_side_effects=True, vmem_limit_bytes=64 << 20
        ),
    )(voltages, steering, chirp_phase, delays)


def solution(mesh):
    in_specs = (P("chan", "tm", None), P("chan", None, None), P("chan", None), P())
    out_specs = P("chan", None, None, "tm")
    return jax.shard_map(local, mesh=mesh, in_specs=in_specs, out_specs=out_specs, check_vma=False)
```

```python
import math

import jax
import jax.numpy as jnp
from jax import lax
from jax.experimental import pallas as pl
from jax.experimental.pallas import tpu as pltpu
from jax.sharding import PartitionSpec as P

MESH = pl.DeviceIdType.MESH
F32 = jnp.float32
BF16 = jnp.bfloat16

NX, NZ, NT = 4, 16, 8
NC = NX * NZ
BEAMS = 512
STATIONS = 512
PER = STATIONS // NC
ROWS = 2 * PER
CHANNELS = 64
BLOCK = 384
HALO = 128
WINDOW = 512
FREQ = 128
PHASES = 1024
SPECTRA = 3072
T = 128
PARTS = BLOCK // T
SHARE = BEAMS // NC
OWNERS = ((0, NZ // 4), (NZ // 4, NZ))
SLABS = len(OWNERS)
XROWS = tuple((end - start) * SHARE for start, end in OWNERS)
SIZE = tuple(NX * rows for rows in XROWS)
FIRST = tuple(sum(SIZE[:i]) for i in range(SLABS))
TILES = tuple(size // 128 for size in SIZE)
QUARTER = NZ // 4 * SHARE
GROUPS = 4
REACH = 4
NEAR = NX * (2 * REACH + 1)
MEMBERS = NC // GROUPS
EPSILON = 1e-06
THIRD = (2, 0, 1)


def shift_of(i):
    j = 15 - (i >> 2)
    half = (j + 1) >> 1
    dz = (NZ // 2 + half * (1 - 2 * (j & 1))) & (NZ - 1)
    return i & (NX - 1), dz


def sincos(turns, period):
    quarter = ((turns + period / 8) * (4.0 / period)).astype(jnp.int32)
    t = (turns - quarter.astype(F32) * (period / 4)) * (2.0 * math.pi / period)
    t2 = t * t
    s = t * (1.0 + t2 * (-1 / 6 + t2 * (1 / 120 + t2 * (-1 / 5040 + t2 * (1 / 362880)))))
    c = 1.0 + t2 * (-1 / 2 + t2 * (1 / 24 + t2 * (-1 / 720 + t2 * (1 / 40320 - t2 * (1 / 3628800)))))
    odd = (quarter & 1) == 1
    cos_part = jnp.where(odd, s, c)
    sin_part = jnp.where(odd, c, s)
    cos_part = jnp.where(((quarter + 1) & 2) == 2, -cos_part, cos_part)
    sin_part = jnp.where((quarter & 2) == 2, -sin_part, sin_part)
    return cos_part, sin_part


def modulo(value, period):
    return value - jnp.floor((value + 0.5) * (1.0 / period)) * period


def iota(shape, dim):
    return lax.broadcasted_iota(jnp.int32, shape, dim)


def halves(x):
    high = x.astype(BF16)
    return high, (x - high.astype(F32)).astype(BF16)


def dot(a, b):
    return jnp.dot(a, b, preferred_element_type=F32)


def dot_rows(a, b):
    return lax.dot_general(a, b, (((1,), (1,)), ((), ())), preferred_element_type=F32)


def kernel(
    volt, steer, chirp, delays, zbuf,
    vbuf, sbuf, cbuf, dbuf, send, recv, w_hi, w_lo, h_hi, h_lo, g_hi, g_lo, gsum,
    acc, last, halo, beams, stat_s, stat_r, columns_of, spec, xbuf_0, xbuf_1, ybuf,
    ready, in_sem, send_sem, recv_sem, halo_sem, stat_ssem, stat_rsem, x_ssem, x_rsem, z_sem,
):
    xbuf = (xbuf_0, xbuf_1)
    me = lax.axis_index("chan")
    mt = lax.axis_index("tm")
    mx, mz = me // NZ, lax.rem(me, NZ)

    loads = [
        pltpu.make_async_copy(volt.at[:, pl.ds(THIRD[p] * T, T), :], vbuf.at[p], in_sem.at[p])
        for p in range(PARTS)
    ]
    loads += [
        pltpu.make_async_copy(steer.at[0], sbuf, in_sem.at[PARTS]),
        pltpu.make_async_copy(chirp, cbuf, in_sem.at[PARTS + 1]),
        pltpu.make_async_copy(delays, dbuf, in_sem.at[PARTS + 2]),
    ]
    for load in loads:
        load.start()

    barrier = pltpu.get_barrier_semaphore()

    def peer(i):
        dx, dz = shift_of(i)
        return ((mx + dx) & (NX - 1)) * NZ + ((mz + dz) & (NZ - 1))

    def greet_chan(i, _):
        pl.semaphore_signal(barrier, inc=1, device_id={"chan": peer(i)}, device_id_type=MESH)
        return 0

    def relative(i):
        dx, dt = ((i >> 3) + 1) & (NX - 1), ((i & (NT - 1)) + 1) & (NT - 1)
        return {"chan": ((mx + dx) & (NX - 1)) * NZ + mz, "tm": (mt + dt) & (NT - 1)}

    def greet_row(i, _):
        @pl.when((i & (NT - 1)) != NT - 1)
        def _():
            pl.semaphore_signal(barrier, inc=1, device_id=relative(i), device_id_type=MESH)

        return 0

    lax.fori_loop(1, NEAR, greet_chan, 0)
    lax.fori_loop(0, NX * NT - 1, greet_row, 0)

    row, col = iota((2 * CHANNELS, 2 * CHANNELS), 0), iota((2 * CHANNELS, 2 * CHANNELS), 1)
    turns = ((row >> 1) * (col & (CHANNELS - 1))) & (CHANNELS - 1)
    tc, ts = sincos(turns.astype(F32), CHANNELS)
    imag_out, imag_in = (row & 1) == 1, col >= CHANNELS
    table = jnp.where(imag_out == imag_in, tc, jnp.where(imag_out, -ts, ts))
    t_hi, t_lo = halves(table * (1.0 / math.sqrt(CHANNELS)))

    def channelise(p):
        loads[p].wait()
        v_hi, v_lo = halves(vbuf[p].reshape(PER * T, 2 * CHANNELS))
        made = dot_rows(t_hi, v_hi) + dot_rows(t_hi, v_lo) + dot_rows(t_lo, v_hi)
        for s in range(PER):
            send[p, pl.ds(s, 2 * CHANNELS, stride=PER), :] = made[:, s * T : (s + 1) * T]

    def rows_of(c):
        return pl.ds(pl.multiple_of(c * ROWS, ROWS), ROWS)

    def give(p, i):
        c = peer(i)
        pltpu.make_async_remote_copy(
            src_ref=send.at[p, rows_of(c), :],
            dst_ref=recv.at[p, rows_of(i), :],
            send_sem=send_sem.at[p],
            recv_sem=recv_sem.at[p, i // MEMBERS],
            device_id={"chan": c},
            device_id_type=MESH,
        ).start()

    def turn(p, first, end):
        def one(i, _):
            give(p, i)
            return 0

        lax.fori_loop(first, end, one, 0)

    def turn_back(p):
        def one(i, _):
            give(p, NC - 1 - i)
            return 0

        lax.fori_loop(0, NC - 1, one, 0)

    def all_but_own(ref, p):
        return ref.at[p, pl.ds(0, (NC - 1) * ROWS), :]

    with jax.named_scope("channelise"):
        channelise(0)
    with jax.named_scope("greeting"):
        pl.semaphore_wait(barrier, NEAR - 1 + NX * (NT - 1))
        for dz in (REACH, NZ - REACH):
            pl.semaphore_signal(
                ready,
                inc=1,
                device_id={"chan": mx * NZ + ((mz + dz) & (NZ - 1))},
                device_id_type=MESH,
            )
    with jax.named_scope("send"):
        turn(0, 1, NEAR)
        channelise(1)
        pl.semaphore_wait(ready, 2)
        turn(0, NEAR, NC)
        turn_back(1)
        channelise(2)
        turn_back(2)
        for p in range(PARTS):
            recv[p, rows_of(0), :] = send[p, rows_of(me), :]

    with jax.named_scope("steering"):
        loads[PARTS].wait()
        er, ec = iota((STATIONS, 2 * STATIONS), 0), iota((STATIONS, 2 * STATIONS), 1)
        dx, dz = shift_of(ec // ROWS)
        sender = ((mx - dx) & (NX - 1)) * NZ + ((mz - dz) & (NZ - 1))
        spread = (sender * PER + (ec & (PER - 1)) == er).astype(F32).astype(BF16)
        rows = QUARTER

        def weigh(j, _):
            at = pl.multiple_of(j * rows, rows)
            index = sbuf[pl.ds(at, rows), :]
            coarse = dot((index >> 5).astype(F32).astype(BF16), spread)
            fine = dot((index & 31).astype(F32).astype(BF16), spread)
            phase = (coarse * 32.0 + fine).astype(jnp.int32)
            column = iota((rows, 2 * STATIONS), 1)
            phase = (phase + ((column >> 3) & 1) * (PHASES // 4)) & (PHASES - 1)
            wc, ws = sincos(phase.astype(F32), PHASES)
            c_hi, c_lo = halves(wc * (1.0 / math.sqrt(STATIONS)))
            s_hi, s_lo = halves(ws * (1.0 / math.sqrt(STATIONS)))
            x, quarter = j // 4, j & 3
            early = quarter == 0
            size = jnp.where(early, SIZE[0], SIZE[1])
            first = jnp.where(early, x * XROWS[0], 2 * SIZE[0] + x * XROWS[1] + (quarter - 1) * rows)
            real = pl.ds(pl.multiple_of(first, rows), rows)
            imag = pl.ds(pl.multiple_of(first + size, rows), rows)
            w_hi[real, :] = c_hi
            w_lo[real, :] = c_lo
            w_hi[imag, :] = s_hi
            w_lo[imag, :] = s_lo
            return 0

        lax.fori_loop(0, BEAMS // rows, weigh, 0)

    with jax.named_scope("filter"):
        loads[PARTS + 1].wait()
        chirp_row = cbuf[...]
        pair = jnp.where(
            iota((8, WINDOW), 0) == 0,
            jnp.broadcast_to(jnp.cos(chirp_row), (8, WINDOW)),
            jnp.broadcast_to(jnp.sin(chirp_row), (8, WINDOW)),
        )
        turns = (iota((WINDOW, WINDOW), 0) * iota((WINDOW, WINDOW), 1)) & (WINDOW - 1)
        fc, fs = sincos(turns.astype(F32), WINDOW)
        by_cos = jnp.dot(pair, fc, precision=lax.Precision.HIGHEST, preferred_element_type=F32)
        by_sin = jnp.dot(pair, fs, precision=lax.Precision.HIGHEST, preferred_element_type=F32)
        h_re = (by_cos[0:1] - by_sin[1:2]) * (1.0 / WINDOW)
        h_im = (by_sin[0:1] + by_cos[1:2]) * (1.0 / WINDOW)
        for k in range(WINDOW // T):
            def rolled(h):
                full = pltpu.roll(jnp.broadcast_to(h, (T, WINDOW)), k * T, 1, stride=1, stride_axis=0)
                return full[:, HALO:]

            r_hi, r_lo = halves(rolled(h_re))
            i_hi, i_lo = halves(rolled(h_im))
            for ref, re, im in ((h_hi, r_hi, i_hi), (h_lo, r_lo, i_lo)):
                ref[k, 0:T, 0:BLOCK] = re
                ref[k, 0:T, BLOCK:] = im
                ref[k, T:, 0:BLOCK] = -im
                ref[k, T:, BLOCK:] = re

    with jax.named_scope("transform"):
        loads[PARTS + 2].wait()
        own = iota((1, CHANNELS), 1) == me
        delay = jnp.sum(jnp.where(own, dbuf[...], 0).astype(F32), axis=1, keepdims=True)
        shape = (BLOCK, FREQ)
        moved = iota(shape, 0).astype(F32) - delay + BLOCK
        turns = modulo(moved, BLOCK) * (iota(shape, 1) + 1).astype(F32)
        gc, gs = sincos(modulo(turns, BLOCK), BLOCK)
        g = jnp.concatenate([gc, -gs], axis=1) * (1.0 / math.sqrt(BLOCK * CHANNELS))
        gsum[...] = jnp.sum(g, axis=0, keepdims=True)
        g_high, g_low = halves(g)
        g_hi[...] = g_high
        g_lo[...] = g_low

    def pair_rows(i):
        return pl.ds(2 * FIRST[i], 2 * SIZE[i])

    def slab_rows(i):
        return pl.ds(FIRST[i], SIZE[i])

    def x_rows(i, x):
        return pl.ds(pl.multiple_of(FIRST[i] + x * XROWS[i], SHARE), XROWS[i])

    def form(p, into, groups=tuple(range(GROUPS))[::-1], slabs=range(SLABS)):
        for g in groups:
            size = MEMBERS * ROWS
            if 0 in slabs:
                there = recv.at[p, pl.ds(g * size, size - ROWS if g == 0 else size), :]
                pltpu.make_async_copy(there, there, recv_sem.at[p, g]).wait()
            columns = pl.ds(g * size, size)
            r_hi, r_lo = halves(recv[p, columns, :])
            both = jnp.concatenate([r_hi, r_lo], axis=1)
            for i in slabs:
                wide = dot(w_hi[pair_rows(i), columns], both)
                made = wide[:, :T] + wide[:, T:] + dot(w_lo[pair_rows(i), columns], r_hi)
                into[pair_rows(i), :] = made if g == GROUPS - 1 else into[pair_rows(i), :] + made

    def convolve(u, k, i):
        x_hi, x_lo = halves(jnp.concatenate([u[: SIZE[i]], u[SIZE[i] :]], axis=1))
        return dot(x_hi, h_hi[k]) + dot(x_lo, h_hi[k]) + dot(x_hi, h_lo[k])

    with jax.named_scope("beams"):
        form(0, last)
        halo_copy = pltpu.make_async_remote_copy(
            src_ref=last,
            dst_ref=halo,
            send_sem=halo_sem.at[0],
            recv_sem=halo_sem.at[1],
            device_id={"tm": (mt + 1) & (NT - 1)},
            device_id_type=MESH,
        )
        halo_copy.start()
        for i in range(SLABS):
            acc[slab_rows(i), :] = convolve(last[pair_rows(i), :], THIRD[0] + 1, i)
        form(1, beams)
        for i in range(SLABS):
            acc[slab_rows(i), :] += convolve(beams[pair_rows(i), :], THIRD[1] + 1, i)
        halo_copy.wait_recv()
        for i in range(SLABS):
            acc[slab_rows(i), :] += convolve(jnp.where(mt > 0, halo[pair_rows(i), :], 0.0), 0, i)
        form(2, beams, (3, 2, 1))

    def hand_x(i):
        for dx in (2, 1, 3):
            x = (mx + dx) & (NX - 1)
            pltpu.make_async_remote_copy(
                src_ref=spec.at[x_rows(i, x), :],
                dst_ref=xbuf[i].at[mx],
                send_sem=x_ssem.at[i],
                recv_sem=x_rsem.at[i],
                device_id={"chan": x * NZ + mz},
                device_id_type=MESH,
            ).start()
        xbuf[i][mx] = spec[x_rows(i, mx), :]

    def detect(i):
        v = acc[slab_rows(i), :] + convolve(beams[pair_rows(i), :], THIRD[2] + 1, i)
        power = v[:, :BLOCK] * v[:, :BLOCK] + v[:, BLOCK:] * v[:, BLOCK:]
        mean = jnp.sum(power, axis=1, keepdims=True) * (1.0 / BLOCK)
        centred = power - mean
        square = jnp.sum(centred * centred, axis=1, keepdims=True)
        lane = iota((SIZE[i], 128), 1)
        rows = jnp.where(lane == 0, mean, jnp.where(lane == 1, square, 0.0)).T
        for k in range(TILES[i]):
            stat_s[i, k : k + 1, :] = rows[0:1, k * 128 : (k + 1) * 128]
            stat_s[i, 3 + k : 4 + k, :] = rows[1:2, k * 128 : (k + 1) * 128]
        stat_s[i, 6:7, :] = gsum[:, :FREQ]
        stat_s[i, 7:8, :] = gsum[:, FREQ:]
        return centred

    def transform(i, centred):
        c_hi, c_lo = halves(centred)
        spec[slab_rows(i), :] = dot(c_hi, g_hi[...]) + dot(c_lo, g_hi[...]) + dot(c_hi, g_lo[...])

    def hand_stat(i):
        def one(j, _):
            pltpu.make_async_remote_copy(
                src_ref=stat_s.at[i],
                dst_ref=stat_r.at[i, mx * NT + mt],
                send_sem=stat_ssem.at[i],
                recv_sem=stat_rsem.at[i],
                device_id=relative(j),
                device_id_type=MESH,
            ).start()
            return 0

        lax.fori_loop(0, NX * NT - 1, one, 0)
        stat_r[i, mx * NT + mt] = stat_s[i]

    def rest_stat(i):
        return stat_r.at[i, pl.ds(0, NX * NT - 1)]

    def rest_x(i):
        return xbuf[i].at[pl.ds(0, NX - 1)]

    with jax.named_scope("detect"):
        for i in range(SLABS):
            form(2, beams, (0,), (i,))
            centred = detect(i)
            hand_stat(i)
            transform(i, centred)
            hand_x(i)

    with jax.named_scope("drain"):
        for p in range(PARTS):
            pltpu.make_async_copy(all_but_own(send, p), all_but_own(send, p), send_sem.at[p]).wait()
        halo_copy.wait_send()

    def scale_rows(i):
        pltpu.make_async_copy(rest_stat(i), rest_stat(i), stat_rsem.at[i]).wait()
        n = TILES[i]
        lines = [[] for _ in range(n)]
        sums = []
        for x in range(NX):
            stats = [stat_r[i, x * NT + j] for j in range(NT)]
            total = stats[0]
            for j in range(1, NT):
                total = total + stats[j]
            mean = total[0:n] * (1.0 / NT)
            square = total[3 : 3 + n]
            for j in range(NT):
                apart = stats[j][0:n] - mean
                square = square + apart * apart * float(BLOCK)
            scale = lax.rsqrt(square * (1.0 / SPECTRA) + EPSILON)
            own = stat_r[i, x * NT + mt]
            shift = own[0:n] - mean
            for k in range(n):
                lines[k] += [scale[k : k + 1], shift[k : k + 1]]
            sums.append(jnp.concatenate([own[6:7], own[7:8]], axis=1))
        for k in range(n):
            tile = jnp.concatenate(lines[k] + [jnp.zeros((128 - 2 * NX, 128), F32)], axis=0)
            columns_of[pl.ds(FIRST[i] + k * 128, 128), :] = tile.T
        return sums

    def sum_x(i):
        sums = scale_rows(i)
        pltpu.make_async_copy(rest_x(i), rest_x(i), x_rsem.at[i]).wait()
        mine = columns_of[x_rows(i, mx), :]
        total = None
        for x in range(NX):
            shift, scale = mine[:, 2 * x + 1 : 2 * x + 2], mine[:, 2 * x : 2 * x + 1]
            term = (xbuf[i][x] + shift * sums[x]) * scale
            total = term if x == 0 else total + term
        start, end = OWNERS[i]
        ybuf[pl.ds(start * SHARE, XROWS[i]), 0, 0, :] = total[:, :FREQ]
        ybuf[pl.ds(start * SHARE, XROWS[i]), 0, 1, :] = total[:, FREQ:]

        def one(k, _):
            half = (k + 1) >> 1
            z = (mz + NZ // 2 + half * (1 - 2 * (k & 1))) & (NZ - 1)

            @pl.when((z >= start) & (z < end))
            def _():
                pltpu.make_async_remote_copy(
                    src_ref=ybuf.at[pl.ds(pl.multiple_of(z * SHARE, SHARE), SHARE)],
                    dst_ref=zbuf.at[mz],
                    send_sem=z_sem.at[0],
                    recv_sem=z_sem.at[1],
                    device_id={"chan": mx * NZ + z},
                    device_id_type=MESH,
                ).start()

            return 0

        lax.fori_loop(0, NZ - 1, one, 0)

    with jax.named_scope("sum_x"):
        for i in range(SLABS):
            sum_x(i)
        keep = pltpu.make_async_copy(
            ybuf.at[pl.ds(pl.multiple_of(mz * SHARE, SHARE), SHARE)], zbuf.at[mz], in_sem.at[0]
        )
        keep.start()

    with jax.named_scope("sum_z"):
        rest_z = zbuf.at[pl.ds(0, NZ - 1)]
        pltpu.make_async_copy(rest_z, rest_z, z_sem.at[1]).wait()
        keep.wait()
        for i in range(SLABS):
            pltpu.make_async_copy(rest_x(i), rest_x(i), x_ssem.at[i]).wait()
            pltpu.make_async_copy(rest_stat(i), rest_stat(i), stat_ssem.at[i]).wait()
        pltpu.make_async_copy(rest_z, rest_z, z_sem.at[0]).wait()


def local(voltages, steering, chirp_phase, delays):
    vmem, sem = pltpu.VMEM, pltpu.SemaphoreType.DMA
    terms = pl.pallas_call(
        kernel,
        out_shape=jax.ShapeDtypeStruct((NZ, SHARE, 1, 2, FREQ), F32),
        in_specs=[pl.BlockSpec(memory_space=pltpu.HBM)] * 4,
        out_specs=pl.BlockSpec(memory_space=pltpu.HBM),
        scratch_shapes=[
            vmem((PARTS, PER, T, 2 * CHANNELS), F32),
            vmem((BEAMS, STATIONS), jnp.int32),
            vmem((1, WINDOW), F32),
            vmem((1, CHANNELS), jnp.int32),
            vmem((PARTS, NC * ROWS, T), F32),
            vmem((PARTS, NC * ROWS, T), F32),
            vmem((2 * BEAMS, 2 * STATIONS), BF16),
            vmem((2 * BEAMS, 2 * STATIONS), BF16),
            vmem((WINDOW // T, 2 * T, 2 * BLOCK), BF16),
            vmem((WINDOW // T, 2 * T, 2 * BLOCK), BF16),
            vmem((BLOCK, 2 * FREQ), BF16),
            vmem((BLOCK, 2 * FREQ), BF16),
            vmem((1, 2 * FREQ), F32),
            vmem((BEAMS, 2 * BLOCK), F32),
            vmem((2 * BEAMS, T), F32),
            vmem((2 * BEAMS, T), F32),
            vmem((2 * BEAMS, T), F32),
            vmem((SLABS, 8, 128), F32),
            vmem((SLABS, NX * NT, 8, 128), F32),
            vmem((BEAMS, 128), F32),
            vmem((BEAMS, 2 * FREQ), F32),
            vmem((NX, XROWS[0], 2 * FREQ), F32),
            vmem((NX, XROWS[1], 2 * FREQ), F32),
            vmem((NZ * SHARE, 1, 2, FREQ), F32),
            pltpu.SemaphoreType.REGULAR,
            sem((PARTS + 3,)),
            sem((PARTS,)),
            sem((PARTS, GROUPS)),
            sem((2,)),
            sem((SLABS,)),
            sem((SLABS,)),
            sem((SLABS,)),
            sem((SLABS,)),
            sem((2,)),
        ],
        compiler_params=pltpu.CompilerParams(
            collective_id=0, has_side_effects=True, vmem_limit_bytes=64 << 20
        ),
    )(voltages, steering, chirp_phase, delays)
    return jnp.sum(terms, axis=0)


def solution(mesh):
    in_specs = (P("chan", "tm", None), P("chan", None, None), P("chan", None), P())
    out_specs = P("chan", None, None, "tm")
    return jax.shard_map(local, mesh=mesh, in_specs=in_specs, out_specs=out_specs, check_vma=False)
```

```python
import math

import jax
import jax.numpy as jnp
from jax import lax
from jax.experimental import pallas as pl
from jax.experimental.pallas import tpu as pltpu
from jax.sharding import PartitionSpec as P

MESH = pl.DeviceIdType.MESH
F32 = jnp.float32
BF16 = jnp.bfloat16

NX, NZ, NT = 4, 16, 8
NC = NX * NZ
BEAMS = 512
STATIONS = 512
PER = STATIONS // NC
ROWS = 2 * PER
CHANNELS = 64
BLOCK = 384
HALO = 128
WINDOW = 512
FREQ = 128
PHASES = 1024
SPECTRA = 3072
T = 128
PARTS = BLOCK // T
SHARE = BEAMS // NC
OWNERS = ((0, NZ // 4), (NZ // 4, NZ))
SLABS = len(OWNERS)
XROWS = tuple((end - start) * SHARE for start, end in OWNERS)
SIZE = tuple(NX * rows for rows in XROWS)
FIRST = tuple(sum(SIZE[:i]) for i in range(SLABS))
TILES = tuple(size // 128 for size in SIZE)
QUARTER = NZ // 4 * SHARE
GROUPS = 4
REACH = 4
NEAR = NX * (2 * REACH + 1)
MEMBERS = NC // GROUPS
EPSILON = 1e-06
THIRD = (2, 0, 1)


def shift_of(i):
    j = 15 - (i >> 2)
    half = (j + 1) >> 1
    dz = (NZ // 2 + half * (1 - 2 * (j & 1))) & (NZ - 1)
    return i & (NX - 1), dz


def sincos(turns, period):
    quarter = ((turns + period / 8) * (4.0 / period)).astype(jnp.int32)
    t = (turns - quarter.astype(F32) * (period / 4)) * (2.0 * math.pi / period)
    t2 = t * t
    s = t * (1.0 + t2 * (-1 / 6 + t2 * (1 / 120 + t2 * (-1 / 5040 + t2 * (1 / 362880)))))
    c = 1.0 + t2 * (-1 / 2 + t2 * (1 / 24 + t2 * (-1 / 720 + t2 * (1 / 40320 - t2 * (1 / 3628800)))))
    odd = (quarter & 1) == 1
    cos_part = jnp.where(odd, s, c)
    sin_part = jnp.where(odd, c, s)
    cos_part = jnp.where(((quarter + 1) & 2) == 2, -cos_part, cos_part)
    sin_part = jnp.where((quarter & 2) == 2, -sin_part, sin_part)
    return cos_part, sin_part


def modulo(value, period):
    return value - jnp.floor((value + 0.5) * (1.0 / period)) * period


def iota(shape, dim):
    return lax.broadcasted_iota(jnp.int32, shape, dim)


def halves(x):
    high = x.astype(BF16)
    return high, (x - high.astype(F32)).astype(BF16)


def dot(a, b):
    return jnp.dot(a, b, preferred_element_type=F32)


def dot_rows(a, b):
    return lax.dot_general(a, b, (((1,), (1,)), ((), ())), preferred_element_type=F32)


def kernel(
    volt, steer, chirp, delays, zbuf,
    vbuf, sbuf, cbuf, dbuf, send, recv, w_hi, w_lo, h_hi, h_lo, g_hi, g_lo, gsum,
    acc, last, halo, beams, stat_s0, stat_s1, stat_r0, stat_r1, columns_of, spec, xbuf_0, xbuf_1, ybuf,
    ready, in_sem, send_sem, recv_sem, halo_sem, stat_ssem, stat_rsem, x_ssem, x_rsem, z_sem,
):
    xbuf = (xbuf_0, xbuf_1)
    stat_s, stat_r = (stat_s0, stat_s1), (stat_r0, stat_r1)
    me = lax.axis_index("chan")
    mt = lax.axis_index("tm")
    mx, mz = me // NZ, lax.rem(me, NZ)

    loads = [
        pltpu.make_async_copy(volt.at[:, pl.ds(THIRD[p] * T, T), :], vbuf.at[p], in_sem.at[p])
        for p in range(PARTS)
    ]
    loads += [
        pltpu.make_async_copy(steer.at[0], sbuf, in_sem.at[PARTS]),
        pltpu.make_async_copy(chirp, cbuf, in_sem.at[PARTS + 1]),
        pltpu.make_async_copy(delays, dbuf, in_sem.at[PARTS + 2]),
    ]
    for load in loads:
        load.start()

    barrier = pltpu.get_barrier_semaphore()

    def peer(i):
        dx, dz = shift_of(i)
        return ((mx + dx) & (NX - 1)) * NZ + ((mz + dz) & (NZ - 1))

    def greet_chan(i, _):
        pl.semaphore_signal(barrier, inc=1, device_id={"chan": peer(i)}, device_id_type=MESH)
        return 0

    def relative(i):
        dx, dt = ((i >> 3) + 1) & (NX - 1), ((i & (NT - 1)) + 1) & (NT - 1)
        return {"chan": ((mx + dx) & (NX - 1)) * NZ + mz, "tm": (mt + dt) & (NT - 1)}

    def greet_row(i, _):
        @pl.when((i & (NT - 1)) != NT - 1)
        def _():
            pl.semaphore_signal(barrier, inc=1, device_id=relative(i), device_id_type=MESH)

        return 0

    lax.fori_loop(1, NEAR, greet_chan, 0)
    lax.fori_loop(0, NX * NT - 1, greet_row, 0)

    row, col = iota((2 * CHANNELS, 2 * CHANNELS), 0), iota((2 * CHANNELS, 2 * CHANNELS), 1)
    turns = ((row >> 1) * (col & (CHANNELS - 1))) & (CHANNELS - 1)
    tc, ts = sincos(turns.astype(F32), CHANNELS)
    imag_out, imag_in = (row & 1) == 1, col >= CHANNELS
    table = jnp.where(imag_out == imag_in, tc, jnp.where(imag_out, -ts, ts))
    t_hi, t_lo = halves(table * (1.0 / math.sqrt(CHANNELS)))

    def channelise(p):
        loads[p].wait()
        v_hi, v_lo = halves(vbuf[p].reshape(PER * T, 2 * CHANNELS))
        made = dot_rows(t_hi, v_hi) + dot_rows(t_hi, v_lo) + dot_rows(t_lo, v_hi)
        for s in range(PER):
            send[p, pl.ds(s, 2 * CHANNELS, stride=PER), :] = made[:, s * T : (s + 1) * T]

    def rows_of(c):
        return pl.ds(pl.multiple_of(c * ROWS, ROWS), ROWS)

    def give(p, i):
        c = peer(i)
        pltpu.make_async_remote_copy(
            src_ref=send.at[p, rows_of(c), :],
            dst_ref=recv.at[p, rows_of(i), :],
            send_sem=send_sem.at[p],
            recv_sem=recv_sem.at[p, i // MEMBERS],
            device_id={"chan": c},
            device_id_type=MESH,
        ).start()

    def turn(p, first, end):
        def one(i, _):
            give(p, i)
            return 0

        lax.fori_loop(first, end, one, 0)

    def turn_back(p):
        def one(i, _):
            give(p, NC - 1 - i)
            return 0

        lax.fori_loop(0, NC - 1, one, 0)

    def all_but_own(ref, p):
        return ref.at[p, pl.ds(0, (NC - 1) * ROWS), :]

    with jax.named_scope("channelise"):
        channelise(0)
    with jax.named_scope("greeting"):
        pl.semaphore_wait(barrier, NEAR - 1 + NX * (NT - 1))
        for dz in (REACH, NZ - REACH):
            pl.semaphore_signal(
                ready,
                inc=1,
                device_id={"chan": mx * NZ + ((mz + dz) & (NZ - 1))},
                device_id_type=MESH,
            )
    with jax.named_scope("send"):
        turn(0, 1, NEAR)
        channelise(1)
        pl.semaphore_wait(ready, 2)
        turn(0, NEAR, NC)
        turn_back(1)
        channelise(2)
        turn_back(2)
        for p in range(PARTS):
            recv[p, rows_of(0), :] = send[p, rows_of(me), :]

    with jax.named_scope("steering"):
        loads[PARTS].wait()
        er, ec = iota((STATIONS, 2 * STATIONS), 0), iota((STATIONS, 2 * STATIONS), 1)
        dx, dz = shift_of(ec // ROWS)
        sender = ((mx - dx) & (NX - 1)) * NZ + ((mz - dz) & (NZ - 1))
        spread = (sender * PER + (ec & (PER - 1)) == er).astype(F32).astype(BF16)
        rows = QUARTER

        def weigh(j, _):
            at = pl.multiple_of(j * rows, rows)
            index = sbuf[pl.ds(at, rows), :]
            coarse = dot((index >> 5).astype(F32).astype(BF16), spread)
            fine = dot((index & 31).astype(F32).astype(BF16), spread)
            phase = (coarse * 32.0 + fine).astype(jnp.int32)
            column = iota((rows, 2 * STATIONS), 1)
            phase = (phase + ((column >> 3) & 1) * (PHASES // 4)) & (PHASES - 1)
            wc, ws = sincos(phase.astype(F32), PHASES)
            c_hi, c_lo = halves(wc * (1.0 / math.sqrt(STATIONS)))
            s_hi, s_lo = halves(ws * (1.0 / math.sqrt(STATIONS)))
            x, quarter = j // 4, j & 3
            early = quarter == 0
            size = jnp.where(early, SIZE[0], SIZE[1])
            first = jnp.where(early, x * XROWS[0], 2 * SIZE[0] + x * XROWS[1] + (quarter - 1) * rows)
            real = pl.ds(pl.multiple_of(first, rows), rows)
            imag = pl.ds(pl.multiple_of(first + size, rows), rows)
            w_hi[real, :] = c_hi
            w_lo[real, :] = c_lo
            w_hi[imag, :] = s_hi
            w_lo[imag, :] = s_lo
            return 0

        lax.fori_loop(0, BEAMS // rows, weigh, 0)

    with jax.named_scope("filter"):
        loads[PARTS + 1].wait()
        chirp_row = cbuf[...]
        pair = jnp.where(
            iota((8, WINDOW), 0) == 0,
            jnp.broadcast_to(jnp.cos(chirp_row), (8, WINDOW)),
            jnp.broadcast_to(jnp.sin(chirp_row), (8, WINDOW)),
        )
        turns = (iota((WINDOW, WINDOW), 0) * iota((WINDOW, WINDOW), 1)) & (WINDOW - 1)
        fc, fs = sincos(turns.astype(F32), WINDOW)
        by_cos = jnp.dot(pair, fc, precision=lax.Precision.HIGHEST, preferred_element_type=F32)
        by_sin = jnp.dot(pair, fs, precision=lax.Precision.HIGHEST, preferred_element_type=F32)
        h_re = (by_cos[0:1] - by_sin[1:2]) * (1.0 / WINDOW)
        h_im = (by_sin[0:1] + by_cos[1:2]) * (1.0 / WINDOW)
        for k in range(WINDOW // T):
            def rolled(h):
                full = pltpu.roll(jnp.broadcast_to(h, (T, WINDOW)), k * T, 1, stride=1, stride_axis=0)
                return full[:, HALO:]

            r_hi, r_lo = halves(rolled(h_re))
            i_hi, i_lo = halves(rolled(h_im))
            for ref, re, im in ((h_hi, r_hi, i_hi), (h_lo, r_lo, i_lo)):
                ref[k, 0:T, 0:BLOCK] = re
                ref[k, 0:T, BLOCK:] = im
                ref[k, T:, 0:BLOCK] = -im
                ref[k, T:, BLOCK:] = re

    with jax.named_scope("transform"):
        loads[PARTS + 2].wait()
        own = iota((1, CHANNELS), 1) == me
        delay = jnp.sum(jnp.where(own, dbuf[...], 0).astype(F32), axis=1, keepdims=True)
        shape = (BLOCK, FREQ)
        moved = iota(shape, 0).astype(F32) - delay + BLOCK
        turns = modulo(moved, BLOCK) * (iota(shape, 1) + 1).astype(F32)
        gc, gs = sincos(modulo(turns, BLOCK), BLOCK)
        g = jnp.concatenate([gc, -gs], axis=1) * (1.0 / math.sqrt(BLOCK * CHANNELS))
        gsum[...] = jnp.sum(g, axis=0, keepdims=True)
        g_high, g_low = halves(g)
        g_hi[...] = g_high
        g_lo[...] = g_low

    def pair_rows(i):
        return pl.ds(2 * FIRST[i], 2 * SIZE[i])

    def slab_rows(i):
        return pl.ds(FIRST[i], SIZE[i])

    def x_rows(i, x):
        return pl.ds(pl.multiple_of(FIRST[i] + x * XROWS[i], SHARE), XROWS[i])

    def form(p, into, groups=tuple(range(GROUPS))[::-1], slabs=range(SLABS)):
        for g in groups:
            size = MEMBERS * ROWS
            if 0 in slabs:
                there = recv.at[p, pl.ds(g * size, size - ROWS if g == 0 else size), :]
                pltpu.make_async_copy(there, there, recv_sem.at[p, g]).wait()
            columns = pl.ds(g * size, size)
            r_hi, r_lo = halves(recv[p, columns, :])
            both = jnp.concatenate([r_hi, r_lo], axis=1)
            for i in slabs:
                wide = dot(w_hi[pair_rows(i), columns], both)
                made = wide[:, :T] + wide[:, T:] + dot(w_lo[pair_rows(i), columns], r_hi)
                into[pair_rows(i), :] = made if g == GROUPS - 1 else into[pair_rows(i), :] + made

    def convolve(u, k, i):
        x_hi, x_lo = halves(jnp.concatenate([u[: SIZE[i]], u[SIZE[i] :]], axis=1))
        return dot(x_hi, h_hi[k]) + dot(x_lo, h_hi[k]) + dot(x_hi, h_lo[k])

    with jax.named_scope("beams"):
        form(0, last)
        halo_copy = pltpu.make_async_remote_copy(
            src_ref=last,
            dst_ref=halo,
            send_sem=halo_sem.at[0],
            recv_sem=halo_sem.at[1],
            device_id={"tm": (mt + 1) & (NT - 1)},
            device_id_type=MESH,
        )
        halo_copy.start()
        for i in range(SLABS):
            acc[slab_rows(i), :] = convolve(last[pair_rows(i), :], THIRD[0] + 1, i)
        form(1, beams)
        for i in range(SLABS):
            acc[slab_rows(i), :] += convolve(beams[pair_rows(i), :], THIRD[1] + 1, i)
        halo_copy.wait_recv()
        for i in range(SLABS):
            acc[slab_rows(i), :] += convolve(jnp.where(mt > 0, halo[pair_rows(i), :], 0.0), 0, i)
        form(2, beams, (3, 2, 1))

    def hand_x(i):
        for dx in (2, 1, 3):
            x = (mx + dx) & (NX - 1)
            pltpu.make_async_remote_copy(
                src_ref=spec.at[x_rows(i, x), :],
                dst_ref=xbuf[i].at[mx],
                send_sem=x_ssem.at[i],
                recv_sem=x_rsem.at[i],
                device_id={"chan": x * NZ + mz},
                device_id_type=MESH,
            ).start()
        xbuf[i][mx] = spec[x_rows(i, mx), :]

    def detect(i):
        v = acc[slab_rows(i), :] + convolve(beams[pair_rows(i), :], THIRD[2] + 1, i)
        power = v[:, :BLOCK] * v[:, :BLOCK] + v[:, BLOCK:] * v[:, BLOCK:]
        mean = jnp.sum(power, axis=1, keepdims=True) * (1.0 / BLOCK)
        centred = power - mean
        square = jnp.sum(centred * centred, axis=1, keepdims=True)
        lane = iota((SIZE[i], 128), 1)
        rows = jnp.where(lane == 0, mean, jnp.where(lane == 1, square, 0.0)).T
        n = TILES[i]
        for k in range(n):
            stat_s[i][k : k + 1, :] = rows[0:1, k * 128 : (k + 1) * 128]
            stat_s[i][n + k : n + k + 1, :] = rows[1:2, k * 128 : (k + 1) * 128]
        stat_s[i][2 * n : 2 * n + 1, :] = gsum[:, :FREQ]
        stat_s[i][2 * n + 1 :, :] = gsum[:, FREQ:]
        return centred

    def transform(i, centred):
        c_hi, c_lo = halves(centred)
        spec[slab_rows(i), :] = dot(c_hi, g_hi[...]) + dot(c_lo, g_hi[...]) + dot(c_hi, g_lo[...])

    def hand_stat(i):
        def one(j, _):
            pltpu.make_async_remote_copy(
                src_ref=stat_s[i],
                dst_ref=stat_r[i].at[mx * NT + mt],
                send_sem=stat_ssem.at[i],
                recv_sem=stat_rsem.at[i],
                device_id=relative(j),
                device_id_type=MESH,
            ).start()
            return 0

        lax.fori_loop(0, NX * NT - 1, one, 0)
        stat_r[i][mx * NT + mt] = stat_s[i][...]

    def rest_stat(i):
        return stat_r[i].at[pl.ds(0, NX * NT - 1)]

    def rest_x(i):
        return xbuf[i].at[pl.ds(0, NX - 1)]

    with jax.named_scope("detect"):
        for i in range(SLABS):
            form(2, beams, (0,), (i,))
            centred = detect(i)
            hand_stat(i)
            transform(i, centred)
            hand_x(i)

    def scale_rows(i):
        pltpu.make_async_copy(rest_stat(i), rest_stat(i), stat_rsem.at[i]).wait()
        n = TILES[i]
        lines = [[] for _ in range(n)]
        sums = []
        for x in range(NX):
            stats = [stat_r[i][x * NT + j] for j in range(NT)]
            total = stats[0]
            for j in range(1, NT):
                total = total + stats[j]
            mean = total[0:n] * (1.0 / NT)
            square = total[n : 2 * n]
            for j in range(NT):
                apart = stats[j][0:n] - mean
                square = square + apart * apart * float(BLOCK)
            scale = lax.rsqrt(square * (1.0 / SPECTRA) + EPSILON)
            own = stat_r[i][x * NT + mt]
            shift = own[0:n] - mean
            for k in range(n):
                lines[k] += [scale[k : k + 1], shift[k : k + 1]]
            sums.append(jnp.concatenate([own[2 * n : 2 * n + 1], own[2 * n + 1 :]], axis=1))
        for k in range(n):
            tile = jnp.concatenate(lines[k] + [jnp.zeros((128 - 2 * NX, 128), F32)], axis=0)
            columns_of[pl.ds(FIRST[i] + k * 128, 128), :] = tile.T
        return sums

    def sum_x(i):
        sums = scale_rows(i)
        pltpu.make_async_copy(rest_x(i), rest_x(i), x_rsem.at[i]).wait()
        mine = columns_of[x_rows(i, mx), :]
        total = None
        for x in range(NX):
            shift, scale = mine[:, 2 * x + 1 : 2 * x + 2], mine[:, 2 * x : 2 * x + 1]
            term = (xbuf[i][x] + shift * sums[x]) * scale
            total = term if x == 0 else total + term
        start, end = OWNERS[i]
        ybuf[pl.ds(start * SHARE, XROWS[i]), 0, 0, :] = total[:, :FREQ]
        ybuf[pl.ds(start * SHARE, XROWS[i]), 0, 1, :] = total[:, FREQ:]

        def one(k, _):
            half = (k + 1) >> 1
            z = (mz + NZ // 2 + half * (1 - 2 * (k & 1))) & (NZ - 1)

            @pl.when((z >= start) & (z < end))
            def _():
                pltpu.make_async_remote_copy(
                    src_ref=ybuf.at[pl.ds(pl.multiple_of(z * SHARE, SHARE), SHARE)],
                    dst_ref=zbuf.at[mz],
                    send_sem=z_sem.at[0],
                    recv_sem=z_sem.at[1],
                    device_id={"chan": mx * NZ + z},
                    device_id_type=MESH,
                ).start()

            return 0

        lax.fori_loop(0, NZ - 1, one, 0)

    with jax.named_scope("sum_x"):
        for i in range(SLABS):
            sum_x(i)
        keep = pltpu.make_async_copy(
            ybuf.at[pl.ds(pl.multiple_of(mz * SHARE, SHARE), SHARE)], zbuf.at[mz], in_sem.at[0]
        )
        keep.start()

    with jax.named_scope("sum_z"):
        rest_z = zbuf.at[pl.ds(0, NZ - 1)]
        pltpu.make_async_copy(rest_z, rest_z, z_sem.at[1]).wait()
        keep.wait()
        for i in range(SLABS):
            pltpu.make_async_copy(rest_x(i), rest_x(i), x_ssem.at[i]).wait()
            pltpu.make_async_copy(rest_stat(i), rest_stat(i), stat_ssem.at[i]).wait()
        pltpu.make_async_copy(rest_z, rest_z, z_sem.at[0]).wait()
        for p in range(PARTS):
            pltpu.make_async_copy(all_but_own(send, p), all_but_own(send, p), send_sem.at[p]).wait()
        halo_copy.wait_send()


def local(voltages, steering, chirp_phase, delays):
    vmem, sem = pltpu.VMEM, pltpu.SemaphoreType.DMA
    terms = pl.pallas_call(
        kernel,
        out_shape=jax.ShapeDtypeStruct((NZ, SHARE, 1, 2, FREQ), F32),
        in_specs=[pl.BlockSpec(memory_space=pltpu.HBM)] * 4,
        out_specs=pl.BlockSpec(memory_space=pltpu.HBM),
        scratch_shapes=[
            vmem((PARTS, PER, T, 2 * CHANNELS), F32),
            vmem((BEAMS, STATIONS), jnp.int32),
            vmem((1, WINDOW), F32),
            vmem((1, CHANNELS), jnp.int32),
            vmem((PARTS, NC * ROWS, T), F32),
            vmem((PARTS, NC * ROWS, T), F32),
            vmem((2 * BEAMS, 2 * STATIONS), BF16),
            vmem((2 * BEAMS, 2 * STATIONS), BF16),
            vmem((WINDOW // T, 2 * T, 2 * BLOCK), BF16),
            vmem((WINDOW // T, 2 * T, 2 * BLOCK), BF16),
            vmem((BLOCK, 2 * FREQ), BF16),
            vmem((BLOCK, 2 * FREQ), BF16),
            vmem((1, 2 * FREQ), F32),
            vmem((BEAMS, 2 * BLOCK), F32),
            vmem((2 * BEAMS, T), F32),
            vmem((2 * BEAMS, T), F32),
            vmem((2 * BEAMS, T), F32),
            vmem((2 * TILES[0] + 2, 128), F32),
            vmem((2 * TILES[1] + 2, 128), F32),
            vmem((NX * NT, 2 * TILES[0] + 2, 128), F32),
            vmem((NX * NT, 2 * TILES[1] + 2, 128), F32),
            vmem((BEAMS, 128), F32),
            vmem((BEAMS, 2 * FREQ), F32),
            vmem((NX, XROWS[0], 2 * FREQ), F32),
            vmem((NX, XROWS[1], 2 * FREQ), F32),
            vmem((NZ * SHARE, 1, 2, FREQ), F32),
            pltpu.SemaphoreType.REGULAR,
            sem((PARTS + 3,)),
            sem((PARTS,)),
            sem((PARTS, GROUPS)),
            sem((2,)),
            sem((SLABS,)),
            sem((SLABS,)),
            sem((SLABS,)),
            sem((SLABS,)),
            sem((2,)),
        ],
        compiler_params=pltpu.CompilerParams(
            collective_id=0, has_side_effects=True, vmem_limit_bytes=64 << 20
        ),
    )(voltages, steering, chirp_phase, delays)
    return jnp.sum(terms, axis=0)


def solution(mesh):
    in_specs = (P("chan", "tm", None), P("chan", None, None), P("chan", None), P())
    out_specs = P("chan", None, None, "tm")
    return jax.shard_map(local, mesh=mesh, in_specs=in_specs, out_specs=out_specs, check_vma=False)
```

```python
import math

import jax
import jax.numpy as jnp
from jax import lax
from jax.experimental import pallas as pl
from jax.experimental.pallas import tpu as pltpu
from jax.sharding import PartitionSpec as P

MESH = pl.DeviceIdType.MESH
F32 = jnp.float32
BF16 = jnp.bfloat16

NX, NZ, NT = 4, 16, 8
NC = NX * NZ
BEAMS = 512
STATIONS = 512
PER = STATIONS // NC
ROWS = 2 * PER
CHANNELS = 64
BLOCK = 384
HALO = 128
WINDOW = 512
FREQ = 128
PHASES = 1024
SPECTRA = 3072
T = 128
PARTS = BLOCK // T
SHARE = BEAMS // NC
OWNERS = ((0, NZ // 4), (NZ // 4, NZ // 2), (NZ // 2, NZ))
SLABS = len(OWNERS)
XROWS = tuple((end - start) * SHARE for start, end in OWNERS)
SIZE = tuple(NX * rows for rows in XROWS)
FIRST = tuple(sum(SIZE[:i]) for i in range(SLABS))
TILES = tuple(size // 128 for size in SIZE)
QUARTER = NZ // 4 * SHARE
GROUPS = 4
REACH = 4
NEAR = NX * (2 * REACH + 1)
MEMBERS = NC // GROUPS
EPSILON = 1e-06
THIRD = (2, 0, 1)


def shift_of(i):
    j = 15 - (i >> 2)
    half = (j + 1) >> 1
    dz = (NZ // 2 + half * (1 - 2 * (j & 1))) & (NZ - 1)
    return i & (NX - 1), dz


def sincos(turns, period):
    quarter = ((turns + period / 8) * (4.0 / period)).astype(jnp.int32)
    t = (turns - quarter.astype(F32) * (period / 4)) * (2.0 * math.pi / period)
    t2 = t * t
    s = t * (1.0 + t2 * (-1 / 6 + t2 * (1 / 120 + t2 * (-1 / 5040 + t2 * (1 / 362880)))))
    c = 1.0 + t2 * (-1 / 2 + t2 * (1 / 24 + t2 * (-1 / 720 + t2 * (1 / 40320 - t2 * (1 / 3628800)))))
    odd = (quarter & 1) == 1
    cos_part = jnp.where(odd, s, c)
    sin_part = jnp.where(odd, c, s)
    cos_part = jnp.where(((quarter + 1) & 2) == 2, -cos_part, cos_part)
    sin_part = jnp.where((quarter & 2) == 2, -sin_part, sin_part)
    return cos_part, sin_part


def modulo(value, period):
    return value - jnp.floor((value + 0.5) * (1.0 / period)) * period


def iota(shape, dim):
    return lax.broadcasted_iota(jnp.int32, shape, dim)


def halves(x):
    high = x.astype(BF16)
    return high, (x - high.astype(F32)).astype(BF16)


def dot(a, b):
    return jnp.dot(a, b, preferred_element_type=F32)


def dot_rows(a, b):
    return lax.dot_general(a, b, (((1,), (1,)), ((), ())), preferred_element_type=F32)


def kernel(
    volt, steer, chirp, delays, zbuf,
    vbuf, sbuf, cbuf, dbuf, send, recv, w_hi, w_lo, h_hi, h_lo, g_hi, g_lo, gsum,
    acc, last, halo, beams, stat_s0, stat_s1, stat_s2, stat_r0, stat_r1, stat_r2, columns_of, spec, xbuf_0, xbuf_1, xbuf_2, ybuf,
    ready, in_sem, send_sem, recv_sem, halo_sem, stat_ssem, stat_rsem, x_ssem, x_rsem, z_sem,
):
    xbuf = (xbuf_0, xbuf_1, xbuf_2)
    stat_s, stat_r = (stat_s0, stat_s1, stat_s2), (stat_r0, stat_r1, stat_r2)
    me = lax.axis_index("chan")
    mt = lax.axis_index("tm")
    mx, mz = me // NZ, lax.rem(me, NZ)

    loads = [
        pltpu.make_async_copy(volt.at[:, pl.ds(THIRD[p] * T, T), :], vbuf.at[p], in_sem.at[p])
        for p in range(PARTS)
    ]
    loads += [
        pltpu.make_async_copy(steer.at[0], sbuf, in_sem.at[PARTS]),
        pltpu.make_async_copy(chirp, cbuf, in_sem.at[PARTS + 1]),
        pltpu.make_async_copy(delays, dbuf, in_sem.at[PARTS + 2]),
    ]
    for load in loads:
        load.start()

    barrier = pltpu.get_barrier_semaphore()

    def peer(i):
        dx, dz = shift_of(i)
        return ((mx + dx) & (NX - 1)) * NZ + ((mz + dz) & (NZ - 1))

    def greet_chan(i, _):
        pl.semaphore_signal(barrier, inc=1, device_id={"chan": peer(i)}, device_id_type=MESH)
        return 0

    def relative(i):
        dx, dt = ((i >> 3) + 1) & (NX - 1), ((i & (NT - 1)) + 1) & (NT - 1)
        return {"chan": ((mx + dx) & (NX - 1)) * NZ + mz, "tm": (mt + dt) & (NT - 1)}

    def greet_row(i, _):
        @pl.when((i & (NT - 1)) != NT - 1)
        def _():
            pl.semaphore_signal(barrier, inc=1, device_id=relative(i), device_id_type=MESH)

        return 0

    lax.fori_loop(1, NEAR, greet_chan, 0)
    lax.fori_loop(0, NX * NT - 1, greet_row, 0)

    row, col = iota((2 * CHANNELS, 2 * CHANNELS), 0), iota((2 * CHANNELS, 2 * CHANNELS), 1)
    turns = ((row >> 1) * (col & (CHANNELS - 1))) & (CHANNELS - 1)
    tc, ts = sincos(turns.astype(F32), CHANNELS)
    imag_out, imag_in = (row & 1) == 1, col >= CHANNELS
    table = jnp.where(imag_out == imag_in, tc, jnp.where(imag_out, -ts, ts))
    t_hi, t_lo = halves(table * (1.0 / math.sqrt(CHANNELS)))

    def channelise(p):
        loads[p].wait()
        v_hi, v_lo = halves(vbuf[p].reshape(PER * T, 2 * CHANNELS))
        made = dot_rows(t_hi, v_hi) + dot_rows(t_hi, v_lo) + dot_rows(t_lo, v_hi)
        for s in range(PER):
            send[p, pl.ds(s, 2 * CHANNELS, stride=PER), :] = made[:, s * T : (s + 1) * T]

    def rows_of(c):
        return pl.ds(pl.multiple_of(c * ROWS, ROWS), ROWS)

    def give(p, i):
        c = peer(i)
        pltpu.make_async_remote_copy(
            src_ref=send.at[p, rows_of(c), :],
            dst_ref=recv.at[p, rows_of(i), :],
            send_sem=send_sem.at[p],
            recv_sem=recv_sem.at[p, i // MEMBERS],
            device_id={"chan": c},
            device_id_type=MESH,
        ).start()

    def turn(p, first, end):
        def one(i, _):
            give(p, i)
            return 0

        lax.fori_loop(first, end, one, 0)

    def turn_back(p):
        def one(i, _):
            give(p, NC - 1 - i)
            return 0

        lax.fori_loop(0, NC - 1, one, 0)

    def all_but_own(ref, p):
        return ref.at[p, pl.ds(0, (NC - 1) * ROWS), :]

    with jax.named_scope("channelise"):
        channelise(0)
    with jax.named_scope("greeting"):
        pl.semaphore_wait(barrier, NEAR - 1 + NX * (NT - 1))
        for dz in (REACH, NZ - REACH):
            pl.semaphore_signal(
                ready,
                inc=1,
                device_id={"chan": mx * NZ + ((mz + dz) & (NZ - 1))},
                device_id_type=MESH,
            )
    with jax.named_scope("send"):
        turn(0, 1, NEAR)
        channelise(1)
        pl.semaphore_wait(ready, 2)
        turn(0, NEAR, NC)
        turn_back(1)
        channelise(2)
        turn_back(2)
        for p in range(PARTS):
            recv[p, rows_of(0), :] = send[p, rows_of(me), :]

    with jax.named_scope("steering"):
        loads[PARTS].wait()
        er, ec = iota((STATIONS, 2 * STATIONS), 0), iota((STATIONS, 2 * STATIONS), 1)
        dx, dz = shift_of(ec // ROWS)
        sender = ((mx - dx) & (NX - 1)) * NZ + ((mz - dz) & (NZ - 1))
        spread = (sender * PER + (ec & (PER - 1)) == er).astype(F32).astype(BF16)
        rows = QUARTER

        def weigh(j, _):
            at = pl.multiple_of(j * rows, rows)
            index = sbuf[pl.ds(at, rows), :]
            coarse = dot((index >> 5).astype(F32).astype(BF16), spread)
            fine = dot((index & 31).astype(F32).astype(BF16), spread)
            phase = (coarse * 32.0 + fine).astype(jnp.int32)
            column = iota((rows, 2 * STATIONS), 1)
            phase = (phase + ((column >> 3) & 1) * (PHASES // 4)) & (PHASES - 1)
            wc, ws = sincos(phase.astype(F32), PHASES)
            c_hi, c_lo = halves(wc * (1.0 / math.sqrt(STATIONS)))
            s_hi, s_lo = halves(ws * (1.0 / math.sqrt(STATIONS)))
            x, quarter = j // 4, j & 3
            size = jnp.where(quarter < 2, SIZE[0], SIZE[2])
            late = 2 * FIRST[2] + x * XROWS[2] + (quarter - 2) * rows
            first = jnp.where(quarter < 2, 2 * FIRST[1] * quarter + x * XROWS[0], late)
            real = pl.ds(pl.multiple_of(first, rows), rows)
            imag = pl.ds(pl.multiple_of(first + size, rows), rows)
            w_hi[real, :] = c_hi
            w_lo[real, :] = c_lo
            w_hi[imag, :] = s_hi
            w_lo[imag, :] = s_lo
            return 0

        lax.fori_loop(0, BEAMS // rows, weigh, 0)

    with jax.named_scope("filter"):
        loads[PARTS + 1].wait()
        chirp_row = cbuf[...]
        pair = jnp.where(
            iota((8, WINDOW), 0) == 0,
            jnp.broadcast_to(jnp.cos(chirp_row), (8, WINDOW)),
            jnp.broadcast_to(jnp.sin(chirp_row), (8, WINDOW)),
        )
        turns = (iota((WINDOW, WINDOW), 0) * iota((WINDOW, WINDOW), 1)) & (WINDOW - 1)
        fc, fs = sincos(turns.astype(F32), WINDOW)
        by_cos = jnp.dot(pair, fc, precision=lax.Precision.HIGHEST, preferred_element_type=F32)
        by_sin = jnp.dot(pair, fs, precision=lax.Precision.HIGHEST, preferred_element_type=F32)
        h_re = (by_cos[0:1] - by_sin[1:2]) * (1.0 / WINDOW)
        h_im = (by_sin[0:1] + by_cos[1:2]) * (1.0 / WINDOW)
        for k in range(WINDOW // T):
            def rolled(h):
                full = pltpu.roll(jnp.broadcast_to(h, (T, WINDOW)), k * T, 1, stride=1, stride_axis=0)
                return full[:, HALO:]

            r_hi, r_lo = halves(rolled(h_re))
            i_hi, i_lo = halves(rolled(h_im))
            for ref, re, im in ((h_hi, r_hi, i_hi), (h_lo, r_lo, i_lo)):
                ref[k, 0:T, 0:BLOCK] = re
                ref[k, 0:T, BLOCK:] = im
                ref[k, T:, 0:BLOCK] = -im
                ref[k, T:, BLOCK:] = re

    with jax.named_scope("transform"):
        loads[PARTS + 2].wait()
        own = iota((1, CHANNELS), 1) == me
        delay = jnp.sum(jnp.where(own, dbuf[...], 0).astype(F32), axis=1, keepdims=True)
        shape = (BLOCK, FREQ)
        moved = iota(shape, 0).astype(F32) - delay + BLOCK
        turns = modulo(moved, BLOCK) * (iota(shape, 1) + 1).astype(F32)
        gc, gs = sincos(modulo(turns, BLOCK), BLOCK)
        g = jnp.concatenate([gc, -gs], axis=1) * (1.0 / math.sqrt(BLOCK * CHANNELS))
        gsum[...] = jnp.sum(g, axis=0, keepdims=True)
        g_high, g_low = halves(g)
        g_hi[...] = g_high
        g_lo[...] = g_low

    def pair_rows(i):
        return pl.ds(2 * FIRST[i], 2 * SIZE[i])

    def slab_rows(i):
        return pl.ds(FIRST[i], SIZE[i])

    def x_rows(i, x):
        return pl.ds(pl.multiple_of(FIRST[i] + x * XROWS[i], SHARE), XROWS[i])

    def form(p, into, groups=tuple(range(GROUPS))[::-1], slabs=range(SLABS)):
        for g in groups:
            size = MEMBERS * ROWS
            if 0 in slabs:
                there = recv.at[p, pl.ds(g * size, size - ROWS if g == 0 else size), :]
                pltpu.make_async_copy(there, there, recv_sem.at[p, g]).wait()
            columns = pl.ds(g * size, size)
            r_hi, r_lo = halves(recv[p, columns, :])
            both = jnp.concatenate([r_hi, r_lo], axis=1)
            for i in slabs:
                wide = dot(w_hi[pair_rows(i), columns], both)
                made = wide[:, :T] + wide[:, T:] + dot(w_lo[pair_rows(i), columns], r_hi)
                into[pair_rows(i), :] = made if g == GROUPS - 1 else into[pair_rows(i), :] + made

    def convolve(u, k, i):
        x_hi, x_lo = halves(jnp.concatenate([u[: SIZE[i]], u[SIZE[i] :]], axis=1))
        return dot(x_hi, h_hi[k]) + dot(x_lo, h_hi[k]) + dot(x_hi, h_lo[k])

    with jax.named_scope("beams"):
        form(0, last)
        halo_copy = pltpu.make_async_remote_copy(
            src_ref=last,
            dst_ref=halo,
            send_sem=halo_sem.at[0],
            recv_sem=halo_sem.at[1],
            device_id={"tm": (mt + 1) & (NT - 1)},
            device_id_type=MESH,
        )
        halo_copy.start()
        for i in range(SLABS):
            acc[slab_rows(i), :] = convolve(last[pair_rows(i), :], THIRD[0] + 1, i)
        form(1, beams)
        for i in range(SLABS):
            acc[slab_rows(i), :] += convolve(beams[pair_rows(i), :], THIRD[1] + 1, i)
        halo_copy.wait_recv()
        for i in range(SLABS):
            acc[slab_rows(i), :] += convolve(jnp.where(mt > 0, halo[pair_rows(i), :], 0.0), 0, i)
        form(2, beams, (3, 2, 1))

    def hand_x(i):
        for dx in (2, 1, 3):
            x = (mx + dx) & (NX - 1)
            pltpu.make_async_remote_copy(
                src_ref=spec.at[x_rows(i, x), :],
                dst_ref=xbuf[i].at[mx],
                send_sem=x_ssem.at[i],
                recv_sem=x_rsem.at[i],
                device_id={"chan": x * NZ + mz},
                device_id_type=MESH,
            ).start()
        xbuf[i][mx] = spec[x_rows(i, mx), :]

    def detect(i):
        v = acc[slab_rows(i), :] + convolve(beams[pair_rows(i), :], THIRD[2] + 1, i)
        power = v[:, :BLOCK] * v[:, :BLOCK] + v[:, BLOCK:] * v[:, BLOCK:]
        mean = jnp.sum(power, axis=1, keepdims=True) * (1.0 / BLOCK)
        centred = power - mean
        square = jnp.sum(centred * centred, axis=1, keepdims=True)
        lane = iota((SIZE[i], 128), 1)
        rows = jnp.where(lane == 0, mean, jnp.where(lane == 1, square, 0.0)).T
        n = TILES[i]
        for k in range(n):
            stat_s[i][k : k + 1, :] = rows[0:1, k * 128 : (k + 1) * 128]
            stat_s[i][n + k : n + k + 1, :] = rows[1:2, k * 128 : (k + 1) * 128]
        stat_s[i][2 * n : 2 * n + 1, :] = gsum[:, :FREQ]
        stat_s[i][2 * n + 1 :, :] = gsum[:, FREQ:]
        return centred

    def transform(i, centred):
        c_hi, c_lo = halves(centred)
        spec[slab_rows(i), :] = dot(c_hi, g_hi[...]) + dot(c_lo, g_hi[...]) + dot(c_hi, g_lo[...])

    def hand_stat(i):
        def one(j, _):
            pltpu.make_async_remote_copy(
                src_ref=stat_s[i],
                dst_ref=stat_r[i].at[mx * NT + mt],
                send_sem=stat_ssem.at[i],
                recv_sem=stat_rsem.at[i],
                device_id=relative(j),
                device_id_type=MESH,
            ).start()
            return 0

        lax.fori_loop(0, NX * NT - 1, one, 0)
        stat_r[i][mx * NT + mt] = stat_s[i][...]

    def rest_stat(i):
        return stat_r[i].at[pl.ds(0, NX * NT - 1)]

    def rest_x(i):
        return xbuf[i].at[pl.ds(0, NX - 1)]

    with jax.named_scope("detect"):
        for i in range(SLABS):
            form(2, beams, (0,), (i,))
            centred = detect(i)
            hand_stat(i)
            transform(i, centred)
            hand_x(i)

    def scale_rows(i):
        pltpu.make_async_copy(rest_stat(i), rest_stat(i), stat_rsem.at[i]).wait()
        n = TILES[i]
        lines = [[] for _ in range(n)]
        sums = []
        for x in range(NX):
            stats = [stat_r[i][x * NT + j] for j in range(NT)]
            total = stats[0]
            for j in range(1, NT):
                total = total + stats[j]
            mean = total[0:n] * (1.0 / NT)
            square = total[n : 2 * n]
            for j in range(NT):
                apart = stats[j][0:n] - mean
                square = square + apart * apart * float(BLOCK)
            scale = lax.rsqrt(square * (1.0 / SPECTRA) + EPSILON)
            own = stat_r[i][x * NT + mt]
            shift = own[0:n] - mean
            for k in range(n):
                lines[k] += [scale[k : k + 1], shift[k : k + 1]]
            sums.append(jnp.concatenate([own[2 * n : 2 * n + 1], own[2 * n + 1 :]], axis=1))
        for k in range(n):
            tile = jnp.concatenate(lines[k] + [jnp.zeros((128 - 2 * NX, 128), F32)], axis=0)
            columns_of[pl.ds(FIRST[i] + k * 128, 128), :] = tile.T
        return sums

    def sum_x(i):
        sums = scale_rows(i)
        pltpu.make_async_copy(rest_x(i), rest_x(i), x_rsem.at[i]).wait()
        mine = columns_of[x_rows(i, mx), :]
        total = None
        for x in range(NX):
            shift, scale = mine[:, 2 * x + 1 : 2 * x + 2], mine[:, 2 * x : 2 * x + 1]
            term = (xbuf[i][x] + shift * sums[x]) * scale
            total = term if x == 0 else total + term
        start, end = OWNERS[i]
        ybuf[pl.ds(start * SHARE, XROWS[i]), 0, 0, :] = total[:, :FREQ]
        ybuf[pl.ds(start * SHARE, XROWS[i]), 0, 1, :] = total[:, FREQ:]

        def one(k, _):
            half = (k + 1) >> 1
            z = (mz + NZ // 2 + half * (1 - 2 * (k & 1))) & (NZ - 1)

            @pl.when((z >= start) & (z < end))
            def _():
                pltpu.make_async_remote_copy(
                    src_ref=ybuf.at[pl.ds(pl.multiple_of(z * SHARE, SHARE), SHARE)],
                    dst_ref=zbuf.at[mz],
                    send_sem=z_sem.at[0],
                    recv_sem=z_sem.at[1],
                    device_id={"chan": mx * NZ + z},
                    device_id_type=MESH,
                ).start()

            return 0

        lax.fori_loop(0, NZ - 1, one, 0)

    with jax.named_scope("sum_x"):
        for i in range(SLABS):
            sum_x(i)
        keep = pltpu.make_async_copy(
            ybuf.at[pl.ds(pl.multiple_of(mz * SHARE, SHARE), SHARE)], zbuf.at[mz], in_sem.at[0]
        )
        keep.start()

    with jax.named_scope("sum_z"):
        rest_z = zbuf.at[pl.ds(0, NZ - 1)]
        pltpu.make_async_copy(rest_z, rest_z, z_sem.at[1]).wait()
        keep.wait()
        for i in range(SLABS):
            pltpu.make_async_copy(rest_x(i), rest_x(i), x_ssem.at[i]).wait()
            pltpu.make_async_copy(rest_stat(i), rest_stat(i), stat_ssem.at[i]).wait()
        pltpu.make_async_copy(rest_z, rest_z, z_sem.at[0]).wait()
        for p in range(PARTS):
            pltpu.make_async_copy(all_but_own(send, p), all_but_own(send, p), send_sem.at[p]).wait()
        halo_copy.wait_send()


def local(voltages, steering, chirp_phase, delays):
    vmem, sem = pltpu.VMEM, pltpu.SemaphoreType.DMA
    terms = pl.pallas_call(
        kernel,
        out_shape=jax.ShapeDtypeStruct((NZ, SHARE, 1, 2, FREQ), F32),
        in_specs=[pl.BlockSpec(memory_space=pltpu.HBM)] * 4,
        out_specs=pl.BlockSpec(memory_space=pltpu.HBM),
        scratch_shapes=[
            vmem((PARTS, PER, T, 2 * CHANNELS), F32),
            vmem((BEAMS, STATIONS), jnp.int32),
            vmem((1, WINDOW), F32),
            vmem((1, CHANNELS), jnp.int32),
            vmem((PARTS, NC * ROWS, T), F32),
            vmem((PARTS, NC * ROWS, T), F32),
            vmem((2 * BEAMS, 2 * STATIONS), BF16),
            vmem((2 * BEAMS, 2 * STATIONS), BF16),
            vmem((WINDOW // T, 2 * T, 2 * BLOCK), BF16),
            vmem((WINDOW // T, 2 * T, 2 * BLOCK), BF16),
            vmem((BLOCK, 2 * FREQ), BF16),
            vmem((BLOCK, 2 * FREQ), BF16),
            vmem((1, 2 * FREQ), F32),
            vmem((BEAMS, 2 * BLOCK), F32),
            vmem((2 * BEAMS, T), F32),
            vmem((2 * BEAMS, T), F32),
            vmem((2 * BEAMS, T), F32),
            *[vmem((2 * n + 2, 128), F32) for n in TILES],
            *[vmem((NX * NT, 2 * n + 2, 128), F32) for n in TILES],
            vmem((BEAMS, 128), F32),
            vmem((BEAMS, 2 * FREQ), F32),
            *[vmem((NX, rows, 2 * FREQ), F32) for rows in XROWS],
            vmem((NZ * SHARE, 1, 2, FREQ), F32),
            pltpu.SemaphoreType.REGULAR,
            sem((PARTS + 3,)),
            sem((PARTS,)),
            sem((PARTS, GROUPS)),
            sem((2,)),
            sem((SLABS,)),
            sem((SLABS,)),
            sem((SLABS,)),
            sem((SLABS,)),
            sem((2,)),
        ],
        compiler_params=pltpu.CompilerParams(
            collective_id=0, has_side_effects=True, vmem_limit_bytes=64 << 20
        ),
    )(voltages, steering, chirp_phase, delays)
    return jnp.sum(terms, axis=0)


def solution(mesh):
    in_specs = (P("chan", "tm", None), P("chan", None, None), P("chan", None), P())
    out_specs = P("chan", None, None, "tm")
    return jax.shard_map(local, mesh=mesh, in_specs=in_specs, out_specs=out_specs, check_vma=False)
```

```python
import math

import jax
import jax.numpy as jnp
from jax import lax
from jax.experimental import pallas as pl
from jax.experimental.pallas import tpu as pltpu
from jax.sharding import PartitionSpec as P

MESH = pl.DeviceIdType.MESH
F32 = jnp.float32
BF16 = jnp.bfloat16

NX, NZ, NT = 4, 16, 8
NC = NX * NZ
BEAMS = 512
STATIONS = 512
PER = STATIONS // NC
ROWS = 2 * PER
CHANNELS = 64
BLOCK = 384
HALO = 128
WINDOW = 512
FREQ = 128
PHASES = 1024
SPECTRA = 3072
T = 128
PARTS = BLOCK // T
SHARE = BEAMS // NC
OWNERS = ((0, NZ // 4), (NZ // 4, NZ))
SLABS = len(OWNERS)
XROWS = tuple((end - start) * SHARE for start, end in OWNERS)
SIZE = tuple(NX * rows for rows in XROWS)
FIRST = tuple(sum(SIZE[:i]) for i in range(SLABS))
TILES = tuple(size // 128 for size in SIZE)
QUARTER = NZ // 4 * SHARE
GROUPS = 4
REACH = 4
NEAR = NX * (2 * REACH + 1)
MEMBERS = NC // GROUPS
EPSILON = 1e-06
THIRD = (2, 0, 1)


def shift_of(i):
    j = 15 - (i >> 2)
    half = (j + 1) >> 1
    dz = (NZ // 2 + half * (1 - 2 * (j & 1))) & (NZ - 1)
    return i & (NX - 1), dz


def sincos(turns, period):
    quarter = ((turns + period / 8) * (4.0 / period)).astype(jnp.int32)
    t = (turns - quarter.astype(F32) * (period / 4)) * (2.0 * math.pi / period)
    t2 = t * t
    s = t * (1.0 + t2 * (-1 / 6 + t2 * (1 / 120 + t2 * (-1 / 5040 + t2 * (1 / 362880)))))
    c = 1.0 + t2 * (-1 / 2 + t2 * (1 / 24 + t2 * (-1 / 720 + t2 * (1 / 40320 - t2 * (1 / 3628800)))))
    odd = (quarter & 1) == 1
    cos_part = jnp.where(odd, s, c)
    sin_part = jnp.where(odd, c, s)
    cos_part = jnp.where(((quarter + 1) & 2) == 2, -cos_part, cos_part)
    sin_part = jnp.where((quarter & 2) == 2, -sin_part, sin_part)
    return cos_part, sin_part


def modulo(value, period):
    return value - jnp.floor((value + 0.5) * (1.0 / period)) * period


def iota(shape, dim):
    return lax.broadcasted_iota(jnp.int32, shape, dim)


def halves(x):
    high = x.astype(BF16)
    return high, (x - high.astype(F32)).astype(BF16)


def dot(a, b):
    return jnp.dot(a, b, preferred_element_type=F32)


def dot_rows(a, b):
    return lax.dot_general(a, b, (((1,), (1,)), ((), ())), preferred_element_type=F32)


def kernel(
    volt, steer, chirp, delays, zbuf,
    vbuf, sbuf, cbuf, dbuf, send, recv, w_hi, w_lo, h_hi, h_lo, g_hi, g_lo, gsum,
    acc, last, halo, beams, stat_s0, stat_s1, stat_r0, stat_r1, columns_of, spec, xbuf_0, xbuf_1, ybuf,
    ready, in_sem, send_sem, recv_sem, halo_sem, stat_ssem, stat_rsem, x_ssem, x_rsem, z_sem,
):
    xbuf = (xbuf_0, xbuf_1)
    stat_s, stat_r = (stat_s0, stat_s1), (stat_r0, stat_r1)
    me = lax.axis_index("chan")
    mt = lax.axis_index("tm")
    mx, mz = me // NZ, lax.rem(me, NZ)

    loads = [
        pltpu.make_async_copy(volt.at[:, pl.ds(THIRD[p] * T, T), :], vbuf.at[p], in_sem.at[p])
        for p in range(PARTS)
    ]
    loads += [
        pltpu.make_async_copy(steer.at[0], sbuf, in_sem.at[PARTS]),
        pltpu.make_async_copy(chirp, cbuf, in_sem.at[PARTS + 1]),
        pltpu.make_async_copy(delays, dbuf, in_sem.at[PARTS + 2]),
    ]
    for load in loads:
        load.start()

    barrier = pltpu.get_barrier_semaphore()

    def peer(i):
        dx, dz = shift_of(i)
        return ((mx + dx) & (NX - 1)) * NZ + ((mz + dz) & (NZ - 1))

    def greet_chan(i, _):
        pl.semaphore_signal(barrier, inc=1, device_id={"chan": peer(i)}, device_id_type=MESH)
        return 0

    def relative(i):
        dx, dt = ((i >> 3) + 1) & (NX - 1), ((i & (NT - 1)) + 1) & (NT - 1)
        return {"chan": ((mx + dx) & (NX - 1)) * NZ + mz, "tm": (mt + dt) & (NT - 1)}

    def greet_row(i, _):
        @pl.when((i & (NT - 1)) != NT - 1)
        def _():
            pl.semaphore_signal(barrier, inc=1, device_id=relative(i), device_id_type=MESH)

        return 0

    lax.fori_loop(1, NEAR, greet_chan, 0)
    lax.fori_loop(0, NX * NT - 1, greet_row, 0)

    row, col = iota((2 * CHANNELS, 2 * CHANNELS), 0), iota((2 * CHANNELS, 2 * CHANNELS), 1)
    turns = ((row >> 1) * (col & (CHANNELS - 1))) & (CHANNELS - 1)
    tc, ts = sincos(turns.astype(F32), CHANNELS)
    imag_out, imag_in = (row & 1) == 1, col >= CHANNELS
    table = jnp.where(imag_out == imag_in, tc, jnp.where(imag_out, -ts, ts))
    t_hi, t_lo = halves(table * (1.0 / math.sqrt(CHANNELS)))

    def channelise(p):
        loads[p].wait()
        v_hi, v_lo = halves(vbuf[p].reshape(PER * T, 2 * CHANNELS))
        made = dot_rows(t_hi, v_hi) + dot_rows(t_hi, v_lo) + dot_rows(t_lo, v_hi)
        for s in range(PER):
            send[p, pl.ds(s, 2 * CHANNELS, stride=PER), :] = made[:, s * T : (s + 1) * T]

    def rows_of(c):
        return pl.ds(pl.multiple_of(c * ROWS, ROWS), ROWS)

    def give(p, i):
        c = peer(i)
        pltpu.make_async_remote_copy(
            src_ref=send.at[p, rows_of(c), :],
            dst_ref=recv.at[p, rows_of(i), :],
            send_sem=send_sem.at[p],
            recv_sem=recv_sem.at[p, i // MEMBERS],
            device_id={"chan": c},
            device_id_type=MESH,
        ).start()

    def turn(p, first, end):
        def one(i, _):
            give(p, i)
            return 0

        lax.fori_loop(first, end, one, 0)

    def turn_back(p):
        def one(i, _):
            give(p, NC - 1 - i)
            return 0

        lax.fori_loop(0, NC - 1, one, 0)

    def all_but_own(ref, p):
        return ref.at[p, pl.ds(0, (NC - 1) * ROWS), :]

    with jax.named_scope("channelise"):
        channelise(0)
    with jax.named_scope("greeting"):
        pl.semaphore_wait(barrier, NEAR - 1 + NX * (NT - 1))
        for dz in (REACH, NZ - REACH):
            pl.semaphore_signal(
                ready,
                inc=1,
                device_id={"chan": mx * NZ + ((mz + dz) & (NZ - 1))},
                device_id_type=MESH,
            )
    with jax.named_scope("send"):
        turn(0, 1, NEAR)
        channelise(1)
        pl.semaphore_wait(ready, 2)
        turn(0, NEAR, NC)
        turn_back(1)
        channelise(2)
        turn_back(2)
        for p in range(PARTS):
            recv[p, rows_of(0), :] = send[p, rows_of(me), :]

    with jax.named_scope("steering"):
        loads[PARTS].wait()
        er, ec = iota((STATIONS, 2 * STATIONS), 0), iota((STATIONS, 2 * STATIONS), 1)
        dx, dz = shift_of(ec // ROWS)
        sender = ((mx - dx) & (NX - 1)) * NZ + ((mz - dz) & (NZ - 1))
        spread = (sender * PER + (ec & (PER - 1)) == er).astype(F32).astype(BF16)
        rows = QUARTER

        def weigh(j, _):
            at = pl.multiple_of(j * rows, rows)
            index = sbuf[pl.ds(at, rows), :]
            coarse = dot((index >> 5).astype(F32).astype(BF16), spread)
            fine = dot((index & 31).astype(F32).astype(BF16), spread)
            phase = (coarse * 32.0 + fine).astype(jnp.int32)
            column = iota((rows, 2 * STATIONS), 1)
            phase = (phase + ((column >> 3) & 1) * (PHASES // 4)) & (PHASES - 1)
            wc, ws = sincos(phase.astype(F32), PHASES)
            c_hi, c_lo = halves(wc * (1.0 / math.sqrt(STATIONS)))
            s_hi, s_lo = halves(ws * (1.0 / math.sqrt(STATIONS)))
            x, quarter = j // 4, j & 3
            early = quarter == 0
            size = jnp.where(early, SIZE[0], SIZE[1])
            first = jnp.where(early, x * XROWS[0], 2 * SIZE[0] + x * XROWS[1] + (quarter - 1) * rows)
            real = pl.ds(pl.multiple_of(first, rows), rows)
            imag = pl.ds(pl.multiple_of(first + size, rows), rows)
            w_hi[real, :] = c_hi
            w_lo[real, :] = c_lo
            w_hi[imag, :] = s_hi
            w_lo[imag, :] = s_lo
            return 0

        lax.fori_loop(0, BEAMS // rows, weigh, 0)

    with jax.named_scope("filter"):
        loads[PARTS + 1].wait()
        chirp_row = cbuf[...]
        pair = jnp.where(
            iota((8, WINDOW), 0) == 0,
            jnp.broadcast_to(jnp.cos(chirp_row), (8, WINDOW)),
            jnp.broadcast_to(jnp.sin(chirp_row), (8, WINDOW)),
        )
        turns = (iota((WINDOW, WINDOW), 0) * iota((WINDOW, WINDOW), 1)) & (WINDOW - 1)
        fc, fs = sincos(turns.astype(F32), WINDOW)
        by_cos = jnp.dot(pair, fc, precision=lax.Precision.HIGHEST, preferred_element_type=F32)
        by_sin = jnp.dot(pair, fs, precision=lax.Precision.HIGHEST, preferred_element_type=F32)
        h_re = (by_cos[0:1] - by_sin[1:2]) * (1.0 / WINDOW)
        h_im = (by_sin[0:1] + by_cos[1:2]) * (1.0 / WINDOW)
        for k in range(WINDOW // T):
            def rolled(h):
                full = pltpu.roll(jnp.broadcast_to(h, (T, WINDOW)), k * T, 1, stride=1, stride_axis=0)
                return full[:, HALO:]

            r_hi, r_lo = halves(rolled(h_re))
            i_hi, i_lo = halves(rolled(h_im))
            for ref, re, im in ((h_hi, r_hi, i_hi), (h_lo, r_lo, i_lo)):
                ref[k, 0:T, 0:BLOCK] = re
                ref[k, 0:T, BLOCK:] = im
                ref[k, T:, 0:BLOCK] = -im
                ref[k, T:, BLOCK:] = re

    with jax.named_scope("transform"):
        loads[PARTS + 2].wait()
        own = iota((1, CHANNELS), 1) == me
        delay = jnp.sum(jnp.where(own, dbuf[...], 0).astype(F32), axis=1, keepdims=True)
        shape = (BLOCK, FREQ)
        moved = iota(shape, 0).astype(F32) - delay + BLOCK
        turns = modulo(moved, BLOCK) * (iota(shape, 1) + 1).astype(F32)
        gc, gs = sincos(modulo(turns, BLOCK), BLOCK)
        g = jnp.concatenate([gc, -gs], axis=1) * (1.0 / math.sqrt(BLOCK * CHANNELS))
        gsum[...] = jnp.sum(g, axis=0, keepdims=True)
        g_high, g_low = halves(g)
        g_hi[...] = g_high
        g_lo[...] = g_low

    def pair_rows(i):
        return pl.ds(2 * FIRST[i], 2 * SIZE[i])

    def slab_rows(i):
        return pl.ds(FIRST[i], SIZE[i])

    def x_rows(i, x):
        return pl.ds(pl.multiple_of(FIRST[i] + x * XROWS[i], SHARE), XROWS[i])

    def form(p, into, groups=tuple(range(GROUPS))[::-1], slabs=range(SLABS)):
        for g in groups:
            size = MEMBERS * ROWS
            if 0 in slabs:
                there = recv.at[p, pl.ds(g * size, size - ROWS if g == 0 else size), :]
                pltpu.make_async_copy(there, there, recv_sem.at[p, g]).wait()
            columns = pl.ds(g * size, size)
            r_hi, r_lo = halves(recv[p, columns, :])
            both = jnp.concatenate([r_hi, r_lo], axis=1)
            for i in slabs:
                wide = dot(w_hi[pair_rows(i), columns], both)
                made = wide[:, :T] + wide[:, T:] + dot(w_lo[pair_rows(i), columns], r_hi)
                into[pair_rows(i), :] = made if g == GROUPS - 1 else into[pair_rows(i), :] + made

    def convolve(u, k, i):
        x_hi, x_lo = halves(jnp.concatenate([u[: SIZE[i]], u[SIZE[i] :]], axis=1))
        return dot(x_hi, h_hi[k]) + dot(x_lo, h_hi[k]) + dot(x_hi, h_lo[k])

    with jax.named_scope("beams"):
        form(0, last)
        halo_copy = pltpu.make_async_remote_copy(
            src_ref=last,
            dst_ref=halo,
            send_sem=halo_sem.at[0],
            recv_sem=halo_sem.at[1],
            device_id={"tm": (mt + 1) & (NT - 1)},
            device_id_type=MESH,
        )
        halo_copy.start()
        for i in range(SLABS):
            acc[slab_rows(i), :] = convolve(last[pair_rows(i), :], THIRD[0] + 1, i)
        form(1, beams)
        for i in range(SLABS):
            acc[slab_rows(i), :] += convolve(beams[pair_rows(i), :], THIRD[1] + 1, i)
        halo_copy.wait_recv()
        for i in range(SLABS):
            acc[slab_rows(i), :] += convolve(jnp.where(mt > 0, halo[pair_rows(i), :], 0.0), 0, i)
        form(2, beams, (3, 2, 1))

    def hand_x(i):
        for dx in (2, 1, 3):
            x = (mx + dx) & (NX - 1)
            pltpu.make_async_remote_copy(
                src_ref=spec.at[x_rows(i, x), :],
                dst_ref=xbuf[i].at[mx],
                send_sem=x_ssem.at[i],
                recv_sem=x_rsem.at[i],
                device_id={"chan": x * NZ + mz},
                device_id_type=MESH,
            ).start()
        xbuf[i][mx] = spec[x_rows(i, mx), :]

    def detect(i):
        v = acc[slab_rows(i), :] + convolve(beams[pair_rows(i), :], THIRD[2] + 1, i)
        power = v[:, :BLOCK] * v[:, :BLOCK] + v[:, BLOCK:] * v[:, BLOCK:]
        mean = jnp.sum(power, axis=1, keepdims=True) * (1.0 / BLOCK)
        centred = power - mean
        square = jnp.sum(centred * centred, axis=1, keepdims=True)
        lane = iota((SIZE[i], 128), 1)
        rows = jnp.where(lane == 0, mean, jnp.where(lane == 1, square, 0.0)).T
        n = TILES[i]
        for k in range(n):
            stat_s[i][k : k + 1, :] = rows[0:1, k * 128 : (k + 1) * 128]
            stat_s[i][n + k : n + k + 1, :] = rows[1:2, k * 128 : (k + 1) * 128]
        stat_s[i][2 * n : 2 * n + 1, :] = gsum[:, :FREQ]
        stat_s[i][2 * n + 1 :, :] = gsum[:, FREQ:]
        return centred

    def transform(i, centred):
        c_hi, c_lo = halves(centred)
        spec[slab_rows(i), :] = dot(c_hi, g_hi[...]) + dot(c_lo, g_hi[...]) + dot(c_hi, g_lo[...])

    def hand_stat(i):
        def one(j, _):
            pltpu.make_async_remote_copy(
                src_ref=stat_s[i],
                dst_ref=stat_r[i].at[mx * NT + mt],
                send_sem=stat_ssem.at[i],
                recv_sem=stat_rsem.at[i],
                device_id=relative(j),
                device_id_type=MESH,
            ).start()
            return 0

        lax.fori_loop(0, NX * NT - 1, one, 0, unroll=True)
        stat_r[i][mx * NT + mt] = stat_s[i][...]

    def rest_stat(i):
        return stat_r[i].at[pl.ds(0, NX * NT - 1)]

    def rest_x(i):
        return xbuf[i].at[pl.ds(0, NX - 1)]

    with jax.named_scope("detect"):
        for i in range(SLABS):
            form(2, beams, (0,), (i,))
            centred = detect(i)
            hand_stat(i)
            transform(i, centred)
            hand_x(i)

    def scale_rows(i):
        pltpu.make_async_copy(rest_stat(i), rest_stat(i), stat_rsem.at[i]).wait()
        n = TILES[i]
        lines = [[] for _ in range(n)]
        sums = []
        for x in range(NX):
            stats = [stat_r[i][x * NT + j] for j in range(NT)]
            total = stats[0]
            for j in range(1, NT):
                total = total + stats[j]
            mean = total[0:n] * (1.0 / NT)
            square = total[n : 2 * n]
            for j in range(NT):
                apart = stats[j][0:n] - mean
                square = square + apart * apart * float(BLOCK)
            scale = lax.rsqrt(square * (1.0 / SPECTRA) + EPSILON)
            own = stat_r[i][x * NT + mt]
            shift = own[0:n] - mean
            for k in range(n):
                lines[k] += [scale[k : k + 1], shift[k : k + 1]]
            sums.append(jnp.concatenate([own[2 * n : 2 * n + 1], own[2 * n + 1 :]], axis=1))
        for k in range(n):
            tile = jnp.concatenate(lines[k] + [jnp.zeros((128 - 2 * NX, 128), F32)], axis=0)
            columns_of[pl.ds(FIRST[i] + k * 128, 128), :] = tile.T
        return sums

    def sum_x(i):
        sums = scale_rows(i)
        pltpu.make_async_copy(rest_x(i), rest_x(i), x_rsem.at[i]).wait()
        mine = columns_of[x_rows(i, mx), :]
        total = None
        for x in range(NX):
            shift, scale = mine[:, 2 * x + 1 : 2 * x + 2], mine[:, 2 * x : 2 * x + 1]
            term = (xbuf[i][x] + shift * sums[x]) * scale
            total = term if x == 0 else total + term
        start, end = OWNERS[i]
        ybuf[pl.ds(start * SHARE, XROWS[i]), 0, 0, :] = total[:, :FREQ]
        ybuf[pl.ds(start * SHARE, XROWS[i]), 0, 1, :] = total[:, FREQ:]

        def one(k, _):
            half = (k + 1) >> 1
            z = (mz + NZ // 2 + half * (1 - 2 * (k & 1))) & (NZ - 1)

            @pl.when((z >= start) & (z < end))
            def _():
                pltpu.make_async_remote_copy(
                    src_ref=ybuf.at[pl.ds(pl.multiple_of(z * SHARE, SHARE), SHARE)],
                    dst_ref=zbuf.at[mz],
                    send_sem=z_sem.at[0],
                    recv_sem=z_sem.at[1],
                    device_id={"chan": mx * NZ + z},
                    device_id_type=MESH,
                ).start()

            return 0

        lax.fori_loop(0, NZ - 1, one, 0)

    with jax.named_scope("sum_x"):
        for i in range(SLABS):
            sum_x(i)
        keep = pltpu.make_async_copy(
            ybuf.at[pl.ds(pl.multiple_of(mz * SHARE, SHARE), SHARE)], zbuf.at[mz], in_sem.at[0]
        )
        keep.start()

    with jax.named_scope("sum_z"):
        rest_z = zbuf.at[pl.ds(0, NZ - 1)]
        pltpu.make_async_copy(rest_z, rest_z, z_sem.at[1]).wait()
        keep.wait()
        for i in range(SLABS):
            pltpu.make_async_copy(rest_x(i), rest_x(i), x_ssem.at[i]).wait()
            pltpu.make_async_copy(rest_stat(i), rest_stat(i), stat_ssem.at[i]).wait()
        pltpu.make_async_copy(rest_z, rest_z, z_sem.at[0]).wait()
        for p in range(PARTS):
            pltpu.make_async_copy(all_but_own(send, p), all_but_own(send, p), send_sem.at[p]).wait()
        halo_copy.wait_send()


def local(voltages, steering, chirp_phase, delays):
    vmem, sem = pltpu.VMEM, pltpu.SemaphoreType.DMA
    terms = pl.pallas_call(
        kernel,
        out_shape=jax.ShapeDtypeStruct((NZ, SHARE, 1, 2, FREQ), F32),
        in_specs=[pl.BlockSpec(memory_space=pltpu.HBM)] * 4,
        out_specs=pl.BlockSpec(memory_space=pltpu.HBM),
        scratch_shapes=[
            vmem((PARTS, PER, T, 2 * CHANNELS), F32),
            vmem((BEAMS, STATIONS), jnp.int32),
            vmem((1, WINDOW), F32),
            vmem((1, CHANNELS), jnp.int32),
            vmem((PARTS, NC * ROWS, T), F32),
            vmem((PARTS, NC * ROWS, T), F32),
            vmem((2 * BEAMS, 2 * STATIONS), BF16),
            vmem((2 * BEAMS, 2 * STATIONS), BF16),
            vmem((WINDOW // T, 2 * T, 2 * BLOCK), BF16),
            vmem((WINDOW // T, 2 * T, 2 * BLOCK), BF16),
            vmem((BLOCK, 2 * FREQ), BF16),
            vmem((BLOCK, 2 * FREQ), BF16),
            vmem((1, 2 * FREQ), F32),
            vmem((BEAMS, 2 * BLOCK), F32),
            vmem((2 * BEAMS, T), F32),
            vmem((2 * BEAMS, T), F32),
            vmem((2 * BEAMS, T), F32),
            vmem((2 * TILES[0] + 2, 128), F32),
            vmem((2 * TILES[1] + 2, 128), F32),
            vmem((NX * NT, 2 * TILES[0] + 2, 128), F32),
            vmem((NX * NT, 2 * TILES[1] + 2, 128), F32),
            vmem((BEAMS, 128), F32),
            vmem((BEAMS, 2 * FREQ), F32),
            vmem((NX, XROWS[0], 2 * FREQ), F32),
            vmem((NX, XROWS[1], 2 * FREQ), F32),
            vmem((NZ * SHARE, 1, 2, FREQ), F32),
            pltpu.SemaphoreType.REGULAR,
            sem((PARTS + 3,)),
            sem((PARTS,)),
            sem((PARTS, GROUPS)),
            sem((2,)),
            sem((SLABS,)),
            sem((SLABS,)),
            sem((SLABS,)),
            sem((SLABS,)),
            sem((2,)),
        ],
        compiler_params=pltpu.CompilerParams(
            collective_id=0, has_side_effects=True, vmem_limit_bytes=64 << 20
        ),
    )(voltages, steering, chirp_phase, delays)
    return jnp.sum(terms, axis=0)


def solution(mesh):
    in_specs = (P("chan", "tm", None), P("chan", None, None), P("chan", None), P())
    out_specs = P("chan", None, None, "tm")
    return jax.shard_map(local, mesh=mesh, in_specs=in_specs, out_specs=out_specs, check_vma=False)
```
